32 devices in a mesh: batch: 4 (over x, core), seq: 8 (over z, y).
Axes of the slice: x: 2, y: 2, z: 4, core: 2. Of those that a mesh axis runs over, the one named last changes fastest.
Arguments:
- block_input: bfloat16 [8, 1024, 1024], P('batch', 'seq'), may hold values from -6 to 6
- doc_lengths: int32 [8, 8], P('batch'), may hold values from 0 to 1024, as said below
- out_grad: bfloat16 [8, 1024, 1024], P('batch', 'seq'), may hold values from -6 to 6
- joined_weight: bfloat16 [1024, 3072], replicated, may hold values from -0.1875 to 0.1875
- proj_weight: bfloat16 [1024, 1024], replicated, may hold values from -0.75 to 0.75
- expand_weight: bfloat16 [1024, 4096], replicated, may hold values from -0.1875 to 0.1875
- shrink_weight: bfloat16 [4096, 1024], replicated, may hold values from -0.09375 to 0.09375
- joined_left: bfloat16 [1024, 128], replicated, may hold values from -0.1875 to 0.1875
- joined_right: bfloat16 [128, 3072], replicated, may hold values from -0.5 to 0.5
- proj_left: bfloat16 [1024, 128], replicated, may hold values from -0.75 to 0.75
- proj_right: bfloat16 [128, 1024], replicated, may hold values from -0.5 to 0.5
- expand_left: bfloat16 [1024, 128], replicated, may hold values from -0.1875 to 0.1875
- expand_right: bfloat16 [128, 4096], replicated, may hold values from -0.5 to 0.5
- shrink_left: bfloat16 [4096, 128], replicated, may hold values from -0.09375 to 0.09375
- shrink_right: bfloat16 [128, 1024], replicated, may hold values from -0.5 to 0.5
- mixer_gain: float32 [1024], replicated, may hold values from 0.5 to 1.5
- mixer_shift: float32 [1024], replicated, may hold values from -3 to 3
- feed_gain: float32 [1024], replicated, may hold values from 0.5 to 1.5
- feed_shift: float32 [1024], replicated, may hold values from -3 to 3
Outputs:
- output: bfloat16 [8, 1024, 1024], P('batch', 'seq')
- input_grad: bfloat16 [8, 1024, 1024], P('batch', 'seq')
- grad_joined_left: float32 [1024, 128], replicated
- grad_joined_right: float32 [128, 3072], replicated
- grad_proj_left: float32 [1024, 128], replicated
- grad_proj_right: float32 [128, 1024], replicated
- grad_expand_left: float32 [1024, 128], replicated
- grad_expand_right: float32 [128, 4096], replicated
- grad_shrink_left: float32 [4096, 128], replicated
- grad_shrink_right: float32 [128, 1024], replicated
- grad_mixer_gain: float32 [1024], replicated
- grad_mixer_shift: float32 [1024], replicated
- grad_feed_gain: float32 [1024], replicated
- grad_feed_shift: float32 [1024], replicated
The draws below stay inside these ranges and needn't reach their ends.
Inputs may be any that keep to these rules, and one draw needn't show every extreme that they name: `doc_lengths`: each row's lengths add up to 1024; zero entries are empty documents. In every aligned group of 2 rows, one row holds a document that begins before slot 128 and ends after slot 896.
All inputs are finite; a program needn't handle non-finite values.
Results may differ from the reference program's by a relative error of at most 0.029.
Values may be sent and summed in bfloat16 or wider, within the bound.
No kernel may reach another device: no remote copies, remote signals or barrier semaphores. Data moves between devices by JAX's collectives and lax.ppermute only.
A program may use at most 320 MiB of HBM per device.

```python
import jax
import jax.numpy as jnp
from jax import lax

D = 1024
HEADS = 16
FF = 4096
HEAD_DIM = 64
ROT_DIM = 16
RANK = 128
UNIT = 128
ROWS_DEV = 2
SLOT_DEV = 128
ROW = 1024
ROWS = 8
DOCS = 8


def draw_doc_lengths(key, part):
    key = jax.random.fold_in(key, 7)
    level_key, second_key, pick_key, head_key, tail_key = jax.random.split(key, 5)
    levels = jnp.minimum(jax.random.randint(level_key, (ROWS, DOCS), 0, 4), jax.random.randint(second_key, (ROWS, DOCS), 0, 4))
    doc_sizes = UNIT * jnp.left_shift(jnp.ones((ROWS, DOCS), jnp.int32), levels)
    endings = jnp.minimum(jnp.cumsum(doc_sizes, axis=1), ROW)
    column = lax.broadcasted_iota(jnp.int32, (ROWS, DOCS), 1)
    endings = jnp.where(column == DOCS - 1, ROW, endings)
    packed = endings - jnp.concatenate([jnp.zeros((ROWS, 1), jnp.int32), endings[:, :-1]], axis=1)
    chosen = jax.random.randint(pick_key, (ROWS // ROWS_DEV,), 0, ROWS_DEV)
    row_index = jnp.arange(ROWS, dtype=jnp.int32)
    spanning = row_index % ROWS_DEV == jnp.repeat(chosen, ROWS_DEV)
    head_room = jax.random.randint(head_key, (ROWS, 1), 1, SLOT_DEV)
    tail_room = jax.random.randint(tail_key, (ROWS, 1), 1, SLOT_DEV)
    long_row = jnp.where(column == 0, head_room, jnp.where(column == 1, ROW - head_room - tail_room, jnp.where(column == 2, tail_room, 0)))
    whole_row = jnp.where(column == 0, ROW, 0)
    long_row = jnp.where((row_index < ROWS_DEV)[:, None], whole_row, long_row)
    return jnp.where(spanning[:, None], long_row, packed).astype(jnp.int32)


def block_scale(key, dims, cuts, least, top_value):
    level, own = 1.0, jax.random.fold_in(key, 6)
    for position, parts in cuts:
        draws = jnp.exp(jax.random.uniform(jax.random.fold_in(own, position), (parts,), jnp.float32, least / len(cuts), top_value / len(cuts)))
        level = level * jnp.repeat(draws, dims[position] // parts).reshape([-1 if axis == position else 1 for axis in range(len(dims))])
    return level


def noise(own_key, extent, deviation, bound, cuts=(), held_as=jnp.bfloat16):
    level = block_scale(own_key, extent, cuts, -0.22, 0.18) if cuts else 1.0
    entries = jax.random.normal(own_key, extent, jnp.float32) * deviation * level
    return jnp.minimum(jnp.maximum(entries, -bound), bound).astype(held_as)


def setup_inputs(seed: int = 0) -> dict:
    key_list = jax.random.split(jax.random.key(seed), 20)
    return {
        "block_input": noise(key_list[0], (ROWS, ROW, D), 1.0, 6.0, ((0, 4), (1, 8))),
        "doc_lengths": draw_doc_lengths(jax.random.fold_in(key_list[19], 71), 0),
        "out_grad": noise(key_list[2], (ROWS, ROW, D), 1.0, 6.0, ((0, 4), (1, 8))),
        "joined_weight": noise(key_list[3], (D, 3 * D), D ** -0.5, 0.1875),
        "proj_weight": noise(key_list[4], (D, D), (D // 16) ** -0.5, 0.75),
        "expand_weight": noise(key_list[5], (D, FF), D ** -0.5, 0.1875),
        "shrink_weight": noise(key_list[6], (FF, D), FF ** -0.5, 0.09375),
        "joined_left": noise(key_list[7], (D, RANK), D ** -0.5, 0.1875),
        "joined_right": noise(key_list[8], (RANK, 3 * D), RANK ** -0.5, 0.5),
        "proj_left": noise(key_list[9], (D, RANK), (D // 16) ** -0.5, 0.75),
        "proj_right": noise(key_list[10], (RANK, D), RANK ** -0.5, 0.5),
        "expand_left": noise(key_list[11], (D, RANK), D ** -0.5, 0.1875),
        "expand_right": noise(key_list[12], (RANK, FF), RANK ** -0.5, 0.5),
        "shrink_left": noise(key_list[13], (FF, RANK), FF ** -0.5, 0.09375),
        "shrink_right": noise(key_list[14], (RANK, D), RANK ** -0.5, 0.5),
        "mixer_gain": jnp.clip(1.0 + 0.1 * jax.random.normal(key_list[15], (D,), jnp.float32), 0.5, 1.5),
        "mixer_shift": noise(key_list[16], (D,), 0.3, 3.0, (), jnp.float32),
        "feed_gain": jnp.clip(1.0 + 0.1 * jax.random.normal(key_list[17], (D,), jnp.float32), 0.5, 1.5),
        "feed_shift": noise(key_list[18], (D,), 0.3, 3.0, (), jnp.float32),
    }


EPSILON = 1e-05
SCALING = 0.25
NEGATIVE = -1e+30
HIGHEST = lax.Precision.HIGHEST

@jax.custom_vjp
def low(v):
    return lax.optimization_barrier(v.astype(jnp.bfloat16)).astype(jnp.float32)

@jax.custom_vjp
def low_back(v):
    return v

def low_keep(v):
    return (low(v), None)

def low_pass(kept, grad):
    return (grad,)

def back_keep(v):
    return (v, None)

def back_low(kept, grad):
    return (low(grad),)
low.defvjp(low_keep, low_pass)
low_back.defvjp(back_keep, back_low)

def layer_norm(values, gain_vector, shift_vector):
    average = lax.optimization_barrier(jnp.mean(values, axis=-1, keepdims=True))
    centred = values - average
    spread = lax.optimization_barrier(jnp.mean(centred * centred, axis=-1, keepdims=True))
    return centred * lax.rsqrt(spread + EPSILON) * gain_vector + shift_vector

def product(left_side, right_side):
    return jnp.dot(left_side, right_side, precision=HIGHEST)

def adapted(inputs, frozen, left_factor, right_factor):
    low_rank = low(low_back(product(inputs, left_factor)))
    return product(inputs, frozen) + SCALING * product(low_rank, right_factor)

def document_info(lengths_row, places):
    endings = jnp.cumsum(lengths_row)
    passed = places[:, None] >= endings[None, :]
    segment = lax.optimization_barrier(jnp.sum(passed.astype(jnp.int32), axis=1))
    begins = lax.optimization_barrier(jnp.sum(jnp.where(passed, lengths_row[None, :], 0), axis=1))
    return (segment, places - begins)

def rotate(head_values, offsets, direction):
    halfway = ROT_DIM // 2
    frequency = 10000.0 ** (-2.0 * jnp.arange(halfway, dtype=jnp.float32) / ROT_DIM)
    angles = offsets.astype(jnp.float32)[..., None] * frequency
    cosine = jnp.cos(angles)[..., None, :]
    sine_part = direction * jnp.sin(angles)[..., None, :]
    former = head_values[..., :halfway]
    latter = head_values[..., halfway:ROT_DIM]
    return jnp.concatenate([former * cosine - latter * sine_part, latter * cosine + former * sine_part, head_values[..., ROT_DIM:]], axis=-1)

def row_forward(inputs, lengths_row, params, frozen):
    joined_left, joined_right, proj_left, proj_right, expand_left, expand_right, shrink_left, shrink_right, mixer_gain, mixer_shift, feed_gain, feed_shift = params
    joined_weight, proj_weight, expand_weight, shrink_weight = frozen
    mixer_low = low(layer_norm(inputs, mixer_gain, mixer_shift))
    feed_low = low(layer_norm(inputs, feed_gain, feed_shift))
    joined_out = low_back(adapted(mixer_low, joined_weight, joined_left, joined_right))
    length = inputs.shape[0]
    places = jnp.arange(length, dtype=jnp.int32)
    segment, offsets = document_info(lengths_row, places)
    split_heads = joined_out.reshape(length, 3, HEADS, HEAD_DIM)
    query_heads = low(rotate(split_heads[:, 0], offsets, 1.0))
    key_heads = low(rotate(split_heads[:, 1], offsets, 1.0))
    value_heads = low(split_heads[:, 2])
    block_size = min(length, 512)

    def one_block(block_index):
        first_row = (block_index * block_size).astype(jnp.int32)
        query_part = lax.dynamic_slice_in_dim(query_heads, first_row, block_size, 0)
        query_places = lax.dynamic_slice_in_dim(places, first_row, block_size, 0)
        query_segment = lax.dynamic_slice_in_dim(segment, first_row, block_size, 0)
        scores = low_back(jnp.einsum('qhd,khd->hqk', query_part, key_heads, precision=HIGHEST) * 0.125)
        allowed = (query_segment[:, None] == segment[None, :]) & (places[None, :] <= query_places[:, None])
        scores = jnp.where(allowed[None], scores, NEGATIVE)
        row_max = lax.optimization_barrier(jnp.max(scores, axis=-1, keepdims=True))
        weights = jnp.exp(scores - row_max)
        probabilities = weights / lax.optimization_barrier(jnp.sum(weights, axis=-1, keepdims=True))
        return jnp.einsum('hqk,khd->qhd', low(probabilities), value_heads, precision=HIGHEST)
    attention = lax.map(jax.checkpoint(one_block), jnp.arange(length // block_size, dtype=jnp.int32))
    attended = low(low_back(attention.reshape(length, D)))
    expanded = low_back(adapted(feed_low, expand_weight, expand_left, expand_right))
    act_low = low(jax.nn.gelu(expanded, approximate=False))
    projected = adapted(attended, proj_weight, proj_left, proj_right)
    shrunk = adapted(act_low, shrink_weight, shrink_left, shrink_right)
    return inputs + projected + shrunk

def reference(block_input, doc_lengths, out_grad, joined_weight, proj_weight, expand_weight, shrink_weight, joined_left, joined_right, proj_left, proj_right, expand_left, expand_right, shrink_left, shrink_right, mixer_gain, mixer_shift, feed_gain, feed_shift):
    frozen = tuple((member.astype(jnp.float32) for member in (joined_weight, proj_weight, expand_weight, shrink_weight)))
    trainable = tuple((member.astype(jnp.float32) for member in (joined_left, joined_right, proj_left, proj_right, expand_left, expand_right, shrink_left, shrink_right, mixer_gain, mixer_shift, feed_gain, feed_shift)))

    def forward(inputs, params):

        def scan_step(running, row_pair):
            row_inputs, lengths_row = row_pair
            return (running, jax.checkpoint(row_forward)(row_inputs, lengths_row, params, frozen))
        ignored, outputs = lax.scan(scan_step, jnp.zeros((), jnp.float32), (inputs, doc_lengths))
        return outputs
    outputs, pullback = jax.vjp(forward, block_input.astype(jnp.float32), trainable)
    grad_inputs, gradients = pullback(out_grad.astype(jnp.float32))
    grad_joined_left, grad_joined_right, grad_proj_left, grad_proj_right, grad_expand_left, grad_expand_right, grad_shrink_left, grad_shrink_right, grad_mixer_gain, grad_mixer_shift, grad_feed_gain, grad_feed_shift = gradients
    return (outputs.astype(jnp.bfloat16), grad_inputs.astype(jnp.bfloat16), grad_joined_left, grad_joined_right, grad_proj_left, grad_proj_right, grad_expand_left, grad_expand_right, grad_shrink_left, grad_shrink_right, grad_mixer_gain, grad_mixer_shift, grad_feed_gain, grad_feed_shift)
```

```python
from functools import partial

import jax
import jax.numpy as jnp
from jax import lax
from jax.experimental import pallas as pl
from jax.experimental.pallas import tpu as pltpu
from jax.sharding import PartitionSpec as P

D = 1024
FF = 4096
HEADS = 16
HEAD_DIM = 64
ROT_DIM = 16
RANK = 128
PAIR = 128
PAIRS = 8

EPSILON = 1e-05
SCALING = 0.25
NEGATIVE = -1e30
BF = jnp.bfloat16
F32 = jnp.float32
MIB = 1024 * 1024

AT_EXPAND_LEFT = 0
AT_EXPAND_RIGHT = D
AT_SHRINK_LEFT = D + FF
AT_SHRINK_RIGHT = D + 2 * FF
FEED_ROWS = 2 * D + 2 * FF
AT_JOINED_LEFT = 0
AT_JOINED_RIGHT = D
AT_PROJ_LEFT = 4 * D
AT_PROJ_RIGHT = 5 * D
AT_NORMS = 6 * D
LATE_ROWS = 6 * D + 512


def nn(left, right):
    return lax.dot_general(left, right, (((1,), (0,)), ((), ())), preferred_element_type=F32)


def nt(left, right):
    return lax.dot_general(left, right, (((1,), (1,)), ((), ())), preferred_element_type=F32)


def tn(left, right):
    return lax.dot_general(left, right, (((0,), (0,)), ((), ())), preferred_element_type=F32)


def normalised(values):
    average = jnp.mean(values, axis=-1, keepdims=True)
    centred = values - average
    spread = jnp.mean(centred * centred, axis=-1, keepdims=True)
    scale = lax.rsqrt(spread + EPSILON)
    return centred * scale, scale


def turn(values, cosine, sine):
    lane = lax.broadcasted_iota(jnp.int32, values.shape, 1) % HEAD_DIM
    half = ROT_DIM // 2
    partner = jnp.where(lane < half, pltpu.roll(values, PAIR - half, 1), pltpu.roll(values, half, 1))
    return values * cosine + partner * sine


def project_kernel(
    x_ref, g_ref, wq_ref, wk_ref, wv_ref, wp_ref, lj_ref, rq_ref, rk_ref, rv_ref, lp_ref, rp_ref,
    gain_ref, shift_ref, cos_ref, sin_ref, msg_ref, low_ref, rank_ref, u_ref,
):
    @pl.when(pl.program_id(0) == 0)
    def _():
        hat, _ = normalised(x_ref[...].astype(F32))
        u_ref[...] = (hat * gain_ref[...] + shift_ref[...]).astype(BF)
        low_ref[...] = nn(u_ref[...], lj_ref[...]).astype(BF)
        rank_ref[...] = (SCALING * nt(g_ref[...], rp_ref[...])).astype(BF)

    u, low = u_ref[...], low_ref[...]
    cosine, sine = cos_ref[...], sin_ref[...]
    query = nn(u, wq_ref[...]) + SCALING * nn(low, rq_ref[...])
    key = nn(u, wk_ref[...]) + SCALING * nn(low, rk_ref[...])
    value = nn(u, wv_ref[...]) + SCALING * nn(low, rv_ref[...])
    grad = nt(g_ref[...], wp_ref[...]) + nt(rank_ref[...], lp_ref[...])
    rows, slots = msg_ref.shape[1], msg_ref.shape[3]
    for pair in range(msg_ref.shape[0]):
        columns = slice(pair * PAIR, (pair + 1) * PAIR)
        parts = (
            turn(query[:, columns], cosine, sine),
            turn(key[:, columns], cosine, sine),
            value[:, columns],
            grad[:, columns],
        )
        for place, part in enumerate(parts):
            part = part.astype(BF)
            for row in range(rows):
                msg_ref[pair, row, place] = part[row * slots : (row + 1) * slots]


def project(x, g, joined_weight, proj_weight, joined_left, joined_right, proj_left, proj_right,
            gain, shift, cosine, sine, rows):
    tokens = x.shape[0]
    slots = tokens // rows
    width = 256
    steps = D // width
    per = width // PAIR
    whole = lambda shape: pl.BlockSpec(shape, lambda j: (0,) * len(shape))
    column = lambda depth, first: pl.BlockSpec((depth, width), lambda j: (0, first + j))
    return pl.pallas_call(
        project_kernel,
        grid=(steps,),
        in_specs=[
            whole((tokens, D)), whole((tokens, D)),
            column(D, 0), column(D, steps), column(D, 2 * steps),
            pl.BlockSpec((width, D), lambda j: (j, 0)),
            whole((D, RANK)),
            column(RANK, 0), column(RANK, steps), column(RANK, 2 * steps),
            pl.BlockSpec((width, RANK), lambda j: (j, 0)),
            whole((RANK, D)),
            whole((1, D)), whole((1, D)),
            whole((tokens, PAIR)), whole((tokens, PAIR)),
        ],
        out_specs=[
            pl.BlockSpec((per, rows, 4, slots, PAIR), lambda j: (j, 0, 0, 0, 0)),
            whole((tokens, RANK)), whole((tokens, RANK)),
        ],
        out_shape=[
            jax.ShapeDtypeStruct((PAIRS, rows, 4, slots, PAIR), BF),
            jax.ShapeDtypeStruct((tokens, RANK), BF),
            jax.ShapeDtypeStruct((tokens, RANK), BF),
        ],
        scratch_shapes=[pltpu.VMEM((tokens, D), BF)],
        compiler_params=pltpu.CompilerParams(vmem_limit_bytes=24 * MIB),
        cost_estimate=pl.CostEstimate(flops=2 * tokens * D * 5 * D, bytes_accessed=12 * MIB, transcendentals=0),
        name="project",
    )(
        x, g, joined_weight, joined_weight, joined_weight, proj_weight, joined_left,
        joined_right, joined_right, joined_right, proj_left, proj_right, gain, shift, cosine, sine,
    )


def feed_kernel(
    x_ref, g_ref, we_ref, ws_ref, le_ref, re_ref, ls_ref, rs_ref, gain_ref, shift_ref,
    shrunk_ref, gfeed_ref, pack_ref, f_ref, lowe_ref, ranks_ref, lows_ref, ranke_ref,
):
    step = pl.program_id(0)
    width = we_ref.shape[1]

    @pl.when(step == 0)
    def _():
        hat, _ = normalised(x_ref[...].astype(F32))
        f_ref[...] = (hat * gain_ref[...] + shift_ref[...]).astype(BF)
        lowe_ref[...] = nn(f_ref[...], le_ref[...]).astype(BF)
        ranks_ref[...] = (SCALING * nt(g_ref[...], rs_ref[...])).astype(BF)
        lows_ref[...] = jnp.zeros_like(lows_ref)
        ranke_ref[...] = jnp.zeros_like(ranke_ref)
        shrunk_ref[...] = jnp.zeros_like(shrunk_ref)
        gfeed_ref[...] = jnp.zeros_like(gfeed_ref)

    g, f, ranks = g_ref[...], f_ref[...], ranks_ref[...]
    expanded = nn(f, we_ref[...]) + SCALING * nn(lowe_ref[...], re_ref[...])
    bell = 0.5 * (1.0 + lax.erf(expanded * 0.7071067811865476))
    act = (expanded * bell).astype(BF)
    slope = bell + expanded * (0.3989422804014327 * jnp.exp(-0.5 * expanded * expanded))
    lows_ref[...] += nn(act, ls_ref[...])
    shrunk_ref[...] += nn(act, ws_ref[...])
    grad_act = nt(g, ws_ref[...]) + nt(ranks, ls_ref[...])
    grad_expanded = (grad_act * slope).astype(BF)
    gfeed_ref[...] += nt(grad_expanded, we_ref[...])
    ranke_ref[...] += nt(grad_expanded, re_ref[...])
    grad_right = SCALING * tn(lowe_ref[...], grad_expanded)
    for block in range(width // RANK):
        at = pl.multiple_of(AT_EXPAND_RIGHT + step * width + block * RANK, RANK)
        pack_ref[pl.ds(at, RANK), :] = grad_right[:, block * RANK : (block + 1) * RANK].astype(BF)
    at = pl.multiple_of(AT_SHRINK_LEFT + step * width, RANK)
    pack_ref[pl.ds(at, width), :] = tn(act, ranks).astype(BF)

    @pl.when(step == pl.num_programs(0) - 1)
    def _():
        low = lows_ref[...].astype(BF)
        shrunk_ref[...] += SCALING * nn(low, rs_ref[...])
        grad_last = SCALING * tn(low, g)
        for block in range(D // RANK):
            at = AT_SHRINK_RIGHT + block * RANK
            pack_ref[at : at + RANK, :] = grad_last[:, block * RANK : (block + 1) * RANK].astype(BF)
        ranke = (SCALING * ranke_ref[...]).astype(BF)
        gfeed_ref[...] += nt(ranke, le_ref[...])
        pack_ref[AT_EXPAND_LEFT : AT_EXPAND_LEFT + D, :] = tn(f, ranke).astype(BF)


def feed(x, g, expand_weight, shrink_weight, expand_left, expand_right, shrink_left, shrink_right, gain, shift):
    tokens = x.shape[0]
    width = 512
    whole = lambda shape: pl.BlockSpec(shape, lambda j: (0,) * len(shape))
    return pl.pallas_call(
        feed_kernel,
        grid=(FF // width,),
        in_specs=[
            whole((tokens, D)), whole((tokens, D)),
            pl.BlockSpec((D, width), lambda j: (0, j)),
            pl.BlockSpec((width, D), lambda j: (j, 0)),
            whole((D, RANK)),
            pl.BlockSpec((RANK, width), lambda j: (0, j)),
            pl.BlockSpec((width, RANK), lambda j: (j, 0)),
            whole((RANK, D)), whole((1, D)), whole((1, D)),
        ],
        out_specs=[whole((tokens, D)), whole((tokens, D)), whole((FEED_ROWS, RANK))],
        out_shape=[
            jax.ShapeDtypeStruct((tokens, D), F32),
            jax.ShapeDtypeStruct((tokens, D), F32),
            jax.ShapeDtypeStruct((FEED_ROWS, RANK), BF),
        ],
        scratch_shapes=[
            pltpu.VMEM((tokens, D), BF),
            pltpu.VMEM((tokens, RANK), BF), pltpu.VMEM((tokens, RANK), BF),
            pltpu.VMEM((tokens, RANK), F32), pltpu.VMEM((tokens, RANK), F32),
        ],
        compiler_params=pltpu.CompilerParams(vmem_limit_bytes=36 * MIB),
        cost_estimate=pl.CostEstimate(flops=2 * tokens * D * FF * 5, bytes_accessed=24 * MIB, transcendentals=2 * tokens * FF),
        name="feed",
    )(x, g, expand_weight, shrink_weight, expand_left, expand_right, shrink_left, shrink_right, gain, shift)


def attend_kernel(msg_ref, start_ref, cos_ref, sin_ref, out_ref, vt_ref, kt_ref, dk_ref, dv_ref):
    count, _, _, slots, _ = msg_ref.shape
    length = count * slots
    keys = msg_ref[:, 0, 1].reshape(length, PAIR)
    values = msg_ref[:, 0, 2].reshape(length, PAIR)
    kt_ref[...] = keys.T
    vt_ref[...] = values.T
    dk_ref[...] = jnp.zeros_like(dk_ref)
    dv_ref[...] = jnp.zeros_like(dv_ref)
    first_head = lax.broadcasted_iota(jnp.int32, (slots, PAIR), 1) < HEAD_DIM
    none = jnp.zeros((slots, PAIR), BF)

    def both(part):
        return jnp.concatenate([jnp.where(first_head, part, none), jnp.where(first_head, none, part)], axis=0)

    for block in range(count):
        seen = (block + 1) * slots
        query = both(msg_ref[block, 0, 0] * BF(0.125))
        grad = both(msg_ref[block, 0, 3])
        query_t, grad_t = query.T, grad.T
        start = start_ref[0, :, block * slots : (block + 1) * slots]
        start = jnp.concatenate([start, start], axis=1)
        place = block * slots + lax.broadcasted_iota(jnp.int32, (1, slots), 1)
        place = jnp.concatenate([place, place], axis=1)
        scores = nn(keys[:seen], query_t)
        key_place = lax.broadcasted_iota(jnp.int32, scores.shape, 0)
        scores = jnp.where((key_place >= start) & (key_place <= place), scores, NEGATIVE)
        top = jnp.max(scores, axis=0, keepdims=True)
        weights = jnp.exp(scores - top)
        probabilities = weights * (1.0 / jnp.sum(weights, axis=0, keepdims=True))
        low = probabilities.astype(BF)
        out_t = nn(vt_ref[:, :seen], low)
        delta = jnp.sum(out_t * grad_t.astype(F32), axis=0, keepdims=True)
        grad_probs = nn(values[:seen], grad_t)
        grad_scores = (probabilities * (grad_probs - delta)).astype(BF)
        dv_ref[:seen] += nn(low, grad)
        dk_ref[:seen] += nn(grad_scores, query)
        query_grad_t = nn(kt_ref[:, :seen], grad_scores)

        def merge(both_t):
            return jnp.concatenate([both_t[:HEAD_DIM, :slots], both_t[HEAD_DIM:, slots:]], axis=0).T

        cosine = cos_ref[0, block * slots : (block + 1) * slots]
        sine = sin_ref[0, block * slots : (block + 1) * slots]
        out_ref[block, 0, 0] = merge(out_t).astype(BF)
        out_ref[block, 0, 1] = turn(0.125 * merge(query_grad_t), cosine, -sine).astype(BF)
    for block in range(count):
        here = slice(block * slots, (block + 1) * slots)
        out_ref[block, 0, 2] = turn(dk_ref[here], cos_ref[0, here], -sin_ref[0, here]).astype(BF)
        out_ref[block, 0, 3] = dv_ref[here].astype(BF)


def attend(message, starts, cosine, sine):
    count, rows, _, slots, _ = message.shape
    length = count * slots
    block = pl.BlockSpec((count, 1, 4, slots, PAIR), lambda r: (0, r, 0, 0, 0))
    table = pl.BlockSpec((1, length, PAIR), lambda r: (r, 0, 0))
    return pl.pallas_call(
        attend_kernel,
        grid=(rows,),
        in_specs=[block, pl.BlockSpec((1, 1, length), lambda r: (r, 0, 0)), table, table],
        out_specs=block,
        out_shape=jax.ShapeDtypeStruct(message.shape, BF),
        scratch_shapes=[
            pltpu.VMEM((PAIR, length), BF), pltpu.VMEM((PAIR, length), BF),
            pltpu.VMEM((length, PAIR), F32), pltpu.VMEM((length, PAIR), F32),
        ],
        compiler_params=pltpu.CompilerParams(vmem_limit_bytes=40 * MIB),
        cost_estimate=pl.CostEstimate(
            flops=rows * length * length * PAIR * 12, bytes_accessed=8 * MIB, transcendentals=rows * length * length
        ),
        name="attend",
    )(message, starts, cosine, sine)


def finish_kernel(
    msg_ref, x_ref, g_ref, shrunk_ref, gfeed_ref, wp_ref, lp_ref, rp_ref, rankp_ref,
    wj_ref, lj_ref, rj_ref, lowj_ref, mgain_ref, mshift_ref, fgain_ref,
    out_ref, igrad_ref, pack_ref,
):
    pairs, rows, _, slots, _ = msg_ref.shape
    tokens = rows * slots

    def gather(place):
        return jnp.concatenate([msg_ref[pair, :, place].reshape(tokens, PAIR) for pair in range(pairs)], axis=1)

    x = x_ref[...].astype(F32)
    g = g_ref[...]
    hat, scale = normalised(x)
    u = (hat * mgain_ref[...] + mshift_ref[...]).astype(BF)

    def put_right(first, matrix):
        for block in range(matrix.shape[1] // RANK):
            at = first + block * RANK
            pack_ref[at : at + RANK, :] = matrix[:, block * RANK : (block + 1) * RANK].astype(BF)

    joined = jnp.concatenate([gather(1), gather(2), gather(3)], axis=1)
    rank = (SCALING * nt(joined, rj_ref[...])).astype(BF)
    pack_ref[AT_JOINED_LEFT : AT_JOINED_LEFT + D, :] = tn(u, rank).astype(BF)
    put_right(AT_JOINED_RIGHT, SCALING * tn(lowj_ref[...], joined))
    grad_mixer = nt(joined, wj_ref[...]) + nt(rank, lj_ref[...])
    grad_feed = gfeed_ref[...]
    mixer_hat, feed_hat = grad_mixer * hat, grad_feed * hat
    sums = [jnp.sum(v, axis=0, keepdims=True) for v in (mixer_hat, grad_mixer, feed_hat, grad_feed)]
    pieces = [v[:, c * RANK : (c + 1) * RANK] for v in sums for c in range(D // RANK)]
    pack_ref[AT_NORMS : AT_NORMS + 32, :] = jnp.concatenate(pieces, axis=0).astype(BF)
    pack_ref[AT_NORMS + 32 :, :] = jnp.zeros((LATE_ROWS - AT_NORMS - 32, RANK), BF)
    pulled = grad_mixer * mgain_ref[...] + grad_feed * fgain_ref[...]
    along = jnp.mean(pulled * hat, axis=-1, keepdims=True)
    level = jnp.mean(pulled, axis=-1, keepdims=True)
    igrad_ref[...] = (g.astype(F32) + scale * (pulled - level - hat * along)).astype(BF)

    attended = gather(0)
    low = nn(attended, lp_ref[...]).astype(BF)
    projected = nn(attended, wp_ref[...]) + SCALING * nn(low, rp_ref[...])
    out_ref[...] = (x + projected + shrunk_ref[...]).astype(BF)
    pack_ref[AT_PROJ_LEFT : AT_PROJ_LEFT + D, :] = tn(attended, rankp_ref[...]).astype(BF)
    put_right(AT_PROJ_RIGHT, SCALING * tn(low, g))


def finish(message, x, g, shrunk, grad_feed, proj_weight, proj_left, proj_right, rank_proj,
           joined_weight, joined_left, joined_right, low_joined, mixer_gain, mixer_shift, feed_gain):
    tokens = x.shape[0]
    return pl.pallas_call(
        finish_kernel,
        out_shape=[
            jax.ShapeDtypeStruct((tokens, D), BF),
            jax.ShapeDtypeStruct((tokens, D), BF),
            jax.ShapeDtypeStruct((LATE_ROWS, RANK), BF),
        ],
        compiler_params=pltpu.CompilerParams(vmem_limit_bytes=40 * MIB),
        cost_estimate=pl.CostEstimate(flops=2 * tokens * D * 6 * D, bytes_accessed=16 * MIB, transcendentals=0),
        name="finish",
    )(message, x, g, shrunk, grad_feed, proj_weight, proj_left, proj_right, rank_proj,
      joined_weight, joined_left, joined_right, low_joined, mixer_gain, mixer_shift, feed_gain)


def swap(part, bit, size):
    return lax.ppermute(part, ("batch", "seq"), [(i, i ^ bit) for i in range(size)])


def add_low(left, right):
    return (left.astype(F32) + right.astype(F32)).astype(BF)


def summed(packed, order, size):
    me = lax.axis_index("batch") * lax.axis_size("seq") + lax.axis_index("seq")
    for bit in order:
        mine = jnp.where((me & bit) == 0, 0, 1)
        halves = packed.reshape(2, packed.shape[0] // 2, RANK)
        away = lax.dynamic_index_in_dim(halves, 1 - mine, 0, keepdims=False)
        keep = lax.dynamic_index_in_dim(halves, mine, 0, keepdims=False)
        packed = add_low(keep, swap(away, bit, size))
    for bit in reversed(order):
        other = swap(packed, bit, size)
        packed = jnp.where(
            (me & bit) == 0, jnp.concatenate([packed, other]), jnp.concatenate([other, packed])
        )
    return packed


def rows_of(packed, first, count):
    return packed[first : first + count].astype(F32)


def columns_of(packed, first, count):
    blocks = packed[first : first + count].reshape(count // RANK, RANK, RANK)
    return jnp.transpose(blocks, (1, 0, 2)).reshape(RANK, count).astype(F32)


def document_offsets(doc_lengths, places):
    endings = jnp.cumsum(doc_lengths, axis=1)
    passed = places[:, :, None] >= endings[:, None, :]
    begins = jnp.sum(jnp.where(passed, doc_lengths[:, None, :], 0), axis=2)
    return places - begins


def tables(offsets):
    half = ROT_DIM // 2
    frequency = 10000.0 ** (-2.0 * jnp.arange(half, dtype=F32) / ROT_DIM)
    lane = jnp.arange(PAIR) % HEAD_DIM
    per_lane = jnp.where(lane < ROT_DIM, frequency[lane % half], 0.0)
    sign = jnp.where(lane < half, -1.0, jnp.where(lane < ROT_DIM, 1.0, 0.0))
    angles = offsets.astype(F32)[..., None] * per_lane
    return jnp.cos(angles), jnp.sin(angles) * sign


def per_device(
    block_input, doc_lengths, out_grad, joined_weight, proj_weight, expand_weight, shrink_weight,
    joined_left, joined_right, proj_left, proj_right, expand_left, expand_right, shrink_left,
    shrink_right, mixer_gain, mixer_shift, feed_gain, feed_shift,
):
    rows, slots = block_input.shape[:2]
    tokens = rows * slots
    devices, batches = lax.axis_size("seq"), lax.axis_size("batch")
    size = devices * batches
    me = lax.axis_index("seq")
    length = devices * slots
    x = block_input.reshape(tokens, D)
    g = out_grad.reshape(tokens, D)
    mixer_gain, mixer_shift = mixer_gain.reshape(1, D), mixer_shift.reshape(1, D)
    feed_gain, feed_shift = feed_gain.reshape(1, D), feed_shift.reshape(1, D)

    places = me * slots + lax.broadcasted_iota(jnp.int32, (rows, slots), 1)
    cosine, sine = tables(document_offsets(doc_lengths, places))
    message, low_joined, rank_proj = project(
        x, g, joined_weight, proj_weight, joined_left, joined_right, proj_left, proj_right,
        mixer_gain, mixer_shift, cosine.reshape(tokens, PAIR), sine.reshape(tokens, PAIR), rows,
    )

    pair_parts = min(devices, PAIRS)
    row_parts = min(devices // pair_parts, rows)
    head_parts = devices // (pair_parts * row_parts)
    my_rows = rows // row_parts
    lanes = PAIR // head_parts

    def send(units):
        if row_parts * head_parts > 1:
            units = units.reshape(PAIRS, row_parts, my_rows, 4, slots, head_parts, lanes)
            units = jnp.transpose(units, (0, 1, 5, 2, 3, 4, 6))
        units = units.reshape(devices, PAIRS // pair_parts, my_rows, 4, slots, lanes)[:, 0]
        return lax.all_to_all(units, "seq", 0, 0, tiled=True)

    def send_back(units):
        units = lax.all_to_all(units[..., :lanes], "seq", 0, 0, tiled=True)
        if row_parts * head_parts > 1:
            units = units.reshape(PAIRS, row_parts, head_parts, my_rows, 4, slots, lanes)
            units = jnp.transpose(units, (0, 1, 3, 4, 5, 2, 6))
        return units.reshape(PAIRS, rows, 4, slots, PAIR)

    arrived = send(message)
    if lanes < PAIR:
        arrived = jnp.pad(arrived, ((0, 0),) * 4 + ((0, PAIR - lanes),))

    shrunk, grad_feed, feed_pack = feed(
        x, g, expand_weight, shrink_weight, expand_left, expand_right, shrink_left, shrink_right,
        feed_gain, feed_shift,
    )

    whole_places = lax.broadcasted_iota(jnp.int32, (rows, length), 1)
    whole_offsets = document_offsets(doc_lengths, whole_places)
    first_row = ((me // head_parts) % row_parts) * my_rows
    whole_offsets = lax.dynamic_slice_in_dim(whole_offsets, first_row, my_rows, 0)
    starts = (whole_places[:my_rows] - whole_offsets).reshape(my_rows, 1, length)
    whole_cosine, whole_sine = tables(whole_offsets)
    answer = attend(arrived, starts, whole_cosine, whole_sine)
    returned = send_back(answer)

    output, input_grad, late_pack = finish(
        returned, x, g, shrunk, grad_feed, proj_weight, proj_left, proj_right, rank_proj,
        joined_weight, joined_left, joined_right, low_joined, mixer_gain, mixer_shift, feed_gain,
    )

    def bits(first, count):
        return [first << step for step in range(count.bit_length() - 1)]

    order = bits(devices, batches) + bits(1, devices)
    feed_sum = summed(feed_pack, order, size)
    late_sum = summed(late_pack, order, size)
    norms = rows_of(late_sum, AT_NORMS, 32).reshape(4, D)
    return (
        output.reshape(rows, slots, D),
        input_grad.reshape(rows, slots, D),
        rows_of(late_sum, AT_JOINED_LEFT, D),
        columns_of(late_sum, AT_JOINED_RIGHT, 3 * D),
        rows_of(late_sum, AT_PROJ_LEFT, D),
        columns_of(late_sum, AT_PROJ_RIGHT, D),
        rows_of(feed_sum, AT_EXPAND_LEFT, D),
        columns_of(feed_sum, AT_EXPAND_RIGHT, FF),
        rows_of(feed_sum, AT_SHRINK_LEFT, FF),
        columns_of(feed_sum, AT_SHRINK_RIGHT, D),
        norms[0], norms[1], norms[2], norms[3],
    )


def solution(mesh):
    act = P("batch", "seq", None)
    return jax.shard_map(
        per_device,
        mesh=mesh,
        in_specs=(act, P("batch", None), act) + (P(),) * 16,
        out_specs=(act, act) + (P(),) * 12,
        check_vma=False,
    )
```

```python
from functools import partial

import jax
import jax.numpy as jnp
from jax import lax
from jax.experimental import pallas as pl
from jax.experimental.pallas import tpu as pltpu
from jax.sharding import PartitionSpec as P

D = 1024
FF = 4096
HEADS = 16
HEAD_DIM = 64
ROT_DIM = 16
RANK = 128
PAIR = 128
PAIRS = 8

EPSILON = 1e-05
SCALING = 0.25
NEGATIVE = -1e30
BF = jnp.bfloat16
F32 = jnp.float32
MIB = 1024 * 1024
WIDE = 60 * MIB
LITTLE = pl.CostEstimate(flops=1, bytes_accessed=1, transcendentals=0)
MUCH = pl.CostEstimate(flops=2 * 10**11, bytes_accessed=1, transcendentals=0)

FEED_UNITS = {"expand_left": 0, "expand_right": 8, "shrink_left": 40, "shrink_right": 72}
FEED_ROWS = 80 * RANK
PROJ_UNITS = {"proj_left": 0, "proj_right": 8}
PROJ_ROWS = 16 * RANK
LATE_UNITS = {"joined_left": 0, "norms": 8}
LATE_ROWS = 9 * RANK


def nn(left, right):
    return lax.dot_general(left, right, (((1,), (0,)), ((), ())), preferred_element_type=F32)


def nt(left, right):
    return lax.dot_general(left, right, (((1,), (1,)), ((), ())), preferred_element_type=F32)


def tn(left, right):
    return lax.dot_general(left, right, (((0,), (0,)), ((), ())), preferred_element_type=F32)


def normalised(values):
    average = jnp.mean(values, axis=-1, keepdims=True)
    centred = values - average
    spread = jnp.mean(centred * centred, axis=-1, keepdims=True)
    scale = lax.rsqrt(spread + EPSILON)
    return centred * scale, scale


def turn(values, cosine, sine):
    lane = lax.broadcasted_iota(jnp.int32, values.shape, 1) % HEAD_DIM
    half = ROT_DIM // 2
    partner = jnp.where(lane < half, pltpu.roll(values, PAIR - half, 1), pltpu.roll(values, half, 1))
    return values * cosine + partner * sine


def document_starts(doc_ref, row, places):
    ending, begins = jnp.int32(0), jnp.zeros_like(places)
    for entry in range(doc_ref.shape[1]):
        ending = ending + doc_ref[row, entry]
        begins = begins + jnp.where(places >= ending, doc_ref[row, entry], 0)
    return begins


def turning(offsets):
    half = ROT_DIM // 2
    index = lax.broadcasted_iota(jnp.int32, (half, 1), 0)
    frequency = jnp.zeros((half, 1), F32)
    for j in range(half):
        frequency = jnp.where(index == j, 10000.0 ** (-2.0 * j / ROT_DIM), frequency)
    angles = offsets.astype(F32) * frequency
    lane = lax.broadcasted_iota(jnp.int32, (half, PAIR), 1) % HEAD_DIM
    here = (lane < ROT_DIM) & (lane % half == lax.broadcasted_iota(jnp.int32, (half, PAIR), 0))
    spread = jnp.where(here, 1.0, 0.0)
    signed = jnp.where(lane < half, -spread, spread)
    exact = partial(
        lax.dot_general, dimension_numbers=(((0,), (0,)), ((), ())),
        precision=lax.Precision.HIGHEST, preferred_element_type=F32,
    )
    cosine = exact(jnp.cos(angles), spread)
    still = lax.broadcasted_iota(jnp.int32, (1, PAIR), 1) % HEAD_DIM >= ROT_DIM
    return cosine + jnp.where(still, 1.0, 0.0), exact(jnp.sin(angles), signed)


def add_low(left, right):
    return (left.astype(F32) + right.astype(F32)).astype(BF)


def after(value, *others):
    return lax.optimization_barrier((value,) + others)[0] if others else value


class Packing:
    def __init__(self, rows, order, stride=None, first=0):
        self.rows, self.order, self.first = rows, order, first
        self.block = rows // 2 ** len(order)
        self.stride = stride or self.block
        self.piece = max(size for size in (16, 32, 64, 128) if self.block % size == 0 and first % size == 0 and self.stride % size == 0)

    def held(self, stride, first):
        return Packing(self.rows, self.order, stride, first)

    def bits(self, block):
        count = len(self.order)
        return [(block >> (count - 1 - step)) & 1 for step in range(count)]

    def place(self, bits):
        place = 0
        for bit, value in zip(self.order, bits):
            place = place * 2 + (value ^ (lax.shift_right_logical(device_number(), bit) & 1))
        return place

    def pieces(self, unit):
        per = self.block // self.piece
        for part in range(RANK // self.piece):
            piece = unit * (RANK // self.piece) + part
            row = self.place(self.bits(piece // per)) * self.stride + self.first + piece % per * self.piece
            yield part * self.piece, pl.multiple_of(row, 16)

    def put(self, ref, unit, value):
        for first, row in self.pieces(unit):
            ref[pl.ds(row, self.piece), :] = value[first : first + self.piece]

    def get(self, ref, unit):
        return jnp.concatenate([ref[pl.ds(row, self.piece), :] for _, row in self.pieces(unit)], axis=0)

    def put_rows(self, ref, unit, matrix):
        matrix = matrix.astype(BF)
        for step in range(matrix.shape[0] // RANK):
            self.put(ref, unit + step, matrix[step * RANK : (step + 1) * RANK])

    def put_columns(self, ref, unit, matrix):
        matrix = matrix.astype(BF)
        for step in range(matrix.shape[1] // RANK):
            self.put(ref, unit + step, matrix[:, step * RANK : (step + 1) * RANK])


class PairPacking(Packing):
    def __init__(self, order, own, pair_bits, stride=None, first=0):
        self.order, self.own, self.pair_bits = order, own, pair_bits
        self.block = -(-3 * RANK // (16 * 2 ** len(own))) * 16
        self.stride, self.first, self.piece = stride or self.block, first, 16
        self.rows = self.block * 2 ** len(own)

    def held(self, stride, first):
        return PairPacking(self.order, self.own, self.pair_bits, stride, first)

    def pieces(self, unit):
        part, pair = divmod(unit, PAIRS)
        for step in range(RANK // 16):
            row = part * RANK + step * 16
            block, inside = divmod(row, self.block)
            inner = dict(zip(self.own, [(block >> (len(self.own) - 1 - k)) & 1 for k in range(len(self.own))]))
            outer = {bit: (pair >> k) & 1 for k, bit in enumerate(self.pair_bits)}
            bits = [inner[bit] if bit in inner else outer[bit] for bit in self.order]
            at = self.place(bits) * self.stride + self.first + inside
            yield step * 16, pl.multiple_of(at, 16)

    def put_own(self, ref, part, value):
        for step in range(RANK // 16):
            block, inside = divmod(part * RANK + step * 16, self.block)
            place = 0
            for k, bit in enumerate(self.own):
                value_bit = (block >> (len(self.own) - 1 - k)) & 1
                place = place * 2 + (value_bit ^ (lax.shift_right_logical(device_number(), bit) & 1))
            at = pl.multiple_of(place * self.block + inside, 16)
            ref[pl.ds(at, 16), :] = value[step * 16 : (step + 1) * 16]


def device_number():
    return lax.axis_index("batch") * lax.axis_size("seq") + lax.axis_index("seq")


def halve(packed, bit, size, *hold):
    half = packed.shape[0] // 2
    return add_low(packed[:half], after(swap(packed[half:], 1 << bit, size), *hold))


def double(packed, bit, size, *hold):
    return jnp.concatenate([packed, after(swap(packed, 1 << bit, size), *hold)])


def join_kernel(*refs):
    *part_refs, out_ref = refs
    for place, part_ref in enumerate(part_refs):
        rows = part_ref.shape[0]
        out_ref[place * rows : (place + 1) * rows] = part_ref[...]


def join(parts):
    rows = sum(part.shape[0] for part in parts)
    return pl.pallas_call(
        join_kernel,
        out_shape=jax.ShapeDtypeStruct((rows, RANK), BF),
        compiler_params=pltpu.CompilerParams(vmem_limit_bytes=WIDE),
        cost_estimate=LITTLE,
        name="join",
    )(*parts)


def masks(pair):
    return [1 << pair[1], 1 << pair[0], (1 << pair[0]) | (1 << pair[1])]


def quarter(packed, pair, size, *hold):
    blocks = packed.reshape(4, packed.shape[0] // 4, RANK)
    others = [swap(blocks[k + 1], mask, size) for k, mask in enumerate(masks(pair))]
    return add_all(blocks[0], [after(other, *hold) for other in others])


def everyone(packed, pair, size, *hold):
    return [packed] + [after(swap(packed, mask, size), *hold) for mask in masks(pair)]


def add_all(first, others):
    total = first.astype(F32)
    for other in others:
        total = total + other.astype(F32)
    return total.astype(BF)


def project_kernel(
    x_ref, g_ref, wj_ref, wp_ref, lj_ref, rj_ref, lp_ref, rp_ref, gain_ref, shift_ref, doc_ref,
    msg_ref, low_ref, rank_ref, wj_here, wp_here, sems,
):
    rows, slots = msg_ref.shape[1], msg_ref.shape[3]
    third = lambda ref, part: ref.at[:, pl.ds(part * D, D)]
    copies = [pltpu.make_async_copy(wp_ref, wp_here, sems.at[3])] + [
        pltpu.make_async_copy(third(wj_ref, part), third(wj_here, part), sems.at[part]) for part in range(3)
    ]
    for copy in copies:
        copy.start()

    def put(place, matrix):
        matrix = matrix.astype(BF)
        for pair in range(PAIRS):
            for row in range(rows):
                msg_ref[pair, row, place] = matrix[row * slots : (row + 1) * slots, pair * PAIR : (pair + 1) * PAIR]

    g = g_ref[...]
    rank = (SCALING * nt(g, rp_ref[...])).astype(BF)
    rank_ref[...] = rank
    hat, _ = normalised(x_ref[...].astype(F32))
    u = (hat * gain_ref[...] + shift_ref[...]).astype(BF)
    low = nn(u, lj_ref[...]).astype(BF)
    low_ref[...] = low
    places = lax.axis_index("seq") * slots + lax.broadcasted_iota(jnp.int32, (1, slots), 1)
    turns = [turning(places - document_starts(doc_ref, row, places)) for row in range(rows)]
    cosine = jnp.concatenate([pair[0] for pair in turns], axis=0)
    sine = jnp.concatenate([pair[1] for pair in turns], axis=0)
    copies[0].wait()
    put(3, nt(g, wp_here[...]) + nt(rank, lp_ref[...]))
    for part in range(3):
        columns = slice(part * D, (part + 1) * D)
        copies[part + 1].wait()
        result = nn(u, wj_here[:, columns]) + SCALING * nn(low, rj_ref[:, columns])
        if part < 2:
            result = jnp.concatenate(
                [turn(result[:, k * PAIR : (k + 1) * PAIR], cosine, sine) for k in range(PAIRS)], axis=1
            )
        put(part, result)


def project(x, g, joined_weight, proj_weight, joined_left, joined_right, proj_left, proj_right,
            gain, shift, doc_lengths, rows):
    tokens = x.shape[0]
    held = pl.BlockSpec(memory_space=pltpu.VMEM)
    away = pl.BlockSpec(memory_space=pl.ANY)
    return pl.pallas_call(
        project_kernel,
        in_specs=[held, held, away, away] + [held] * 6 + [pl.BlockSpec(memory_space=pltpu.SMEM)],
        out_shape=[
            jax.ShapeDtypeStruct((PAIRS, rows, 4, tokens // rows, PAIR), BF),
            jax.ShapeDtypeStruct((tokens, RANK), BF),
            jax.ShapeDtypeStruct((tokens, RANK), BF),
        ],
        scratch_shapes=[
            pltpu.VMEM((D, 3 * D), BF), pltpu.VMEM((D, D), BF), pltpu.SemaphoreType.DMA((4,)),
        ],
        compiler_params=pltpu.CompilerParams(vmem_limit_bytes=WIDE),
        cost_estimate=LITTLE,
        name="project",
    )(x, g, joined_weight, proj_weight, joined_left, joined_right, proj_left, proj_right, gain, shift, doc_lengths)


def feed_kernel(
    packing, x_ref, g_ref, we_ref, ws_ref, le_ref, re_ref, ls_ref, rs_ref, gain_ref, shift_ref,
    shrunk_ref, gfeed_ref, pack_ref, f_ref, lowe_ref, ranks_ref, lows_ref, ranke_ref,
):
    step = pl.program_id(0)
    width = we_ref.shape[1]

    @pl.when(step == 0)
    def _():
        hat, _ = normalised(x_ref[...].astype(F32))
        f_ref[...] = (hat * gain_ref[...] + shift_ref[...]).astype(BF)
        lowe_ref[...] = nn(f_ref[...], le_ref[...]).astype(BF)
        ranks_ref[...] = (SCALING * nt(g_ref[...], rs_ref[...])).astype(BF)
        lows_ref[...] = jnp.zeros_like(lows_ref)
        ranke_ref[...] = jnp.zeros_like(ranke_ref)
        shrunk_ref[...] = jnp.zeros_like(shrunk_ref)
        gfeed_ref[...] = jnp.zeros_like(gfeed_ref)

    g, f, ranks = g_ref[...], f_ref[...], ranks_ref[...]
    expanded = nn(f, we_ref[...]) + SCALING * nn(lowe_ref[...], re_ref[...])
    bell = 0.5 * (1.0 + lax.erf(expanded * 0.7071067811865476))
    act = (expanded * bell).astype(BF)
    slope = bell + expanded * (0.3989422804014327 * jnp.exp(-0.5 * expanded * expanded))
    lows_ref[...] += nn(act, ls_ref[...])
    shrunk_ref[...] += nn(act, ws_ref[...])
    grad_act = nt(g, ws_ref[...]) + nt(ranks, ls_ref[...])
    grad_expanded = (grad_act * slope).astype(BF)
    gfeed_ref[...] += nt(grad_expanded, we_ref[...])
    ranke_ref[...] += nt(grad_expanded, re_ref[...])
    units = step * (width // RANK)
    packing.put_columns(pack_ref, FEED_UNITS["expand_right"] + units, SCALING * tn(lowe_ref[...], grad_expanded))
    packing.put_rows(pack_ref, FEED_UNITS["shrink_left"] + units, tn(act, ranks))

    @pl.when(step == pl.num_programs(0) - 1)
    def _():
        low = lows_ref[...].astype(BF)
        shrunk_ref[...] += SCALING * nn(low, rs_ref[...])
        packing.put_columns(pack_ref, FEED_UNITS["shrink_right"], SCALING * tn(low, g))
        ranke = (SCALING * ranke_ref[...]).astype(BF)
        gfeed_ref[...] += nt(ranke, le_ref[...])
        packing.put_rows(pack_ref, FEED_UNITS["expand_left"], tn(f, ranke))


def feed(x, g, expand_weight, shrink_weight, expand_left, expand_right, shrink_left, shrink_right, gain, shift, packing):
    tokens = x.shape[0]
    width = 512
    whole = lambda shape: pl.BlockSpec(shape, lambda j: (0,) * len(shape))
    return pl.pallas_call(
        partial(feed_kernel, packing),
        grid=(FF // width,),
        in_specs=[
            whole((tokens, D)), whole((tokens, D)),
            pl.BlockSpec((D, width), lambda j: (0, j)),
            pl.BlockSpec((width, D), lambda j: (j, 0)),
            whole((D, RANK)),
            pl.BlockSpec((RANK, width), lambda j: (0, j)),
            pl.BlockSpec((width, RANK), lambda j: (j, 0)),
            whole((RANK, D)), whole((1, D)), whole((1, D)),
        ],
        out_specs=[whole((tokens, D)), whole((tokens, D)), whole((FEED_ROWS, RANK))],
        out_shape=[
            jax.ShapeDtypeStruct((tokens, D), F32),
            jax.ShapeDtypeStruct((tokens, D), F32),
            jax.ShapeDtypeStruct((FEED_ROWS, RANK), BF),
        ],
        scratch_shapes=[
            pltpu.VMEM((tokens, D), BF),
            pltpu.VMEM((tokens, RANK), BF), pltpu.VMEM((tokens, RANK), BF),
            pltpu.VMEM((tokens, RANK), F32), pltpu.VMEM((tokens, RANK), F32),
        ],
        compiler_params=pltpu.CompilerParams(vmem_limit_bytes=WIDE),
        cost_estimate=LITTLE,
        name="feed",
    )(x, g, expand_weight, shrink_weight, expand_left, expand_right, shrink_left, shrink_right, gain, shift)


def attend_kernel(first_row, my_rows, row_parts, head_parts, msg_ref, doc_ref, *refs):
    out_ref, rest_ref, vt_ref, kt_ref, dk_ref, dv_ref, cos_ref, sin_ref = refs[-8:]
    count, _, _, slots, _ = msg_ref.shape
    length = count * slots
    row = first_row
    if row_parts > 1:
        row = row + (lax.axis_index("seq") // head_parts) % row_parts * my_rows
    places = lax.broadcasted_iota(jnp.int32, (1, length), 1)
    starts = document_starts(doc_ref, row, places)
    cos_ref[...], sin_ref[...] = turning(places - starts)
    keys = msg_ref[:, 0, 1].reshape(length, PAIR)
    values = msg_ref[:, 0, 2].reshape(length, PAIR)
    kt_ref[...] = keys.T
    vt_ref[...] = values.T
    dk_ref[...] = jnp.zeros_like(dk_ref)
    dv_ref[...] = jnp.zeros_like(dv_ref)
    first_head = lax.broadcasted_iota(jnp.int32, (slots, PAIR), 1) < HEAD_DIM
    none = jnp.zeros((slots, PAIR), BF)

    def both(part):
        return jnp.concatenate([jnp.where(first_head, part, none), jnp.where(first_head, none, part)], axis=0)

    def merge(both_t):
        return jnp.concatenate([both_t[:HEAD_DIM, :slots], both_t[HEAD_DIM:, slots:]], axis=0).T

    def front(block):
        here = slice(block * slots, (block + 1) * slots)
        seen = (block + 1) * slots
        query = both(msg_ref[block, 0, 0] * BF(0.125))
        grad = both(msg_ref[block, 0, 3])
        query_t, grad_t = query.T, grad.T
        start = jnp.concatenate([starts[:, here]] * 2, axis=1)
        place = jnp.concatenate([places[:, here]] * 2, axis=1)
        scores = nn(keys[:seen], query_t)
        key_place = lax.broadcasted_iota(jnp.int32, scores.shape, 0)
        allowed = key_place >= start
        if block:
            last = (key_place[-slots:] <= place) & allowed[-slots:]
            scores = jnp.concatenate(
                [jnp.where(allowed[:-slots], scores[:-slots], NEGATIVE), jnp.where(last, scores[-slots:], NEGATIVE)], axis=0
            )
        else:
            scores = jnp.where(allowed & (key_place <= place), scores, NEGATIVE)
        return scores, query, grad_t

    def back(block, scores, query, grad_t):
        here = slice(block * slots, (block + 1) * slots)
        seen = (block + 1) * slots
        top = jnp.max(scores, axis=0, keepdims=True)
        weights = jnp.exp(scores - top)
        inverse = 1.0 / jnp.sum(weights, axis=0, keepdims=True)
        low = weights.astype(BF)
        out_t = nn(vt_ref[:, :seen], low) * inverse
        scaled_t = grad_t.astype(F32) * inverse
        delta = jnp.sum(out_t * scaled_t, axis=0, keepdims=True)
        scaled_t = scaled_t.astype(BF)
        grad_probs = nn(values[:seen], scaled_t)
        grad_scores = (weights * (grad_probs - delta)).astype(BF)
        dv_ref[:seen] += nn(low, scaled_t.T)
        dk_ref[:seen] += nn(grad_scores, query)
        query_grad_t = nn(kt_ref[:, :seen], grad_scores)
        out_ref[block, 0] = merge(out_t).astype(BF)
        query_grad = turn(0.125 * merge(query_grad_t), cos_ref[here], -sin_ref[here])
        rest_ref[block, 0, 0] = query_grad.astype(BF)

    ready = front(0)
    for block in range(count):
        later = front(block + 1) if block + 1 < count else None
        back(block, *ready)
        ready = later
    for block in range(count):
        here = slice(block * slots, (block + 1) * slots)
        rest_ref[block, 0, 1] = turn(dk_ref[here], cos_ref[here], -sin_ref[here]).astype(BF)
        rest_ref[block, 0, 2] = dv_ref[here].astype(BF)


def attend(message, doc_lengths, row, earlier, row_parts, head_parts):
    count, rows, _, slots, _ = message.shape
    length = count * slots
    return pl.pallas_call(
        partial(attend_kernel, row, rows, row_parts, head_parts),
        grid=(1,),
        in_specs=[
            pl.BlockSpec((count, 1, 4, slots, PAIR), lambda r: (0, row, 0, 0, 0)),
            pl.BlockSpec(memory_space=pltpu.SMEM),
        ] + [pl.BlockSpec(memory_space=pl.ANY)] * len(earlier),
        out_specs=[
            pl.BlockSpec((count, 1, slots, PAIR), lambda r: (0, row, 0, 0)),
            pl.BlockSpec((count, 1, 3, slots, PAIR), lambda r: (0, row, 0, 0, 0)),
        ],
        out_shape=[
            jax.ShapeDtypeStruct((count, rows, slots, PAIR), BF),
            jax.ShapeDtypeStruct((count, rows, 3, slots, PAIR), BF),
        ],
        input_output_aliases={2 + k: k for k in range(len(earlier))},
        scratch_shapes=[
            pltpu.VMEM((PAIR, length), BF), pltpu.VMEM((PAIR, length), BF),
            pltpu.VMEM((length, PAIR), F32), pltpu.VMEM((length, PAIR), F32),
            pltpu.VMEM((length, PAIR), F32), pltpu.VMEM((length, PAIR), F32),
        ],
        compiler_params=pltpu.CompilerParams(vmem_limit_bytes=WIDE),
        cost_estimate=LITTLE if row else MUCH,
        name="attend",
    )(message, doc_lengths, *earlier)


def finish_proj_kernel(
    packing, att_ref, x_ref, g_ref, shrunk_ref, wp_ref, lp_ref, rp_ref, rankp_ref, out_ref, pack_ref,
):
    pairs, rows, slots, _ = att_ref.shape
    attended = jnp.concatenate([att_ref[pair].reshape(rows * slots, PAIR) for pair in range(pairs)], axis=1)
    low = nn(attended, lp_ref[...]).astype(BF)
    packing.put_rows(pack_ref, PROJ_UNITS["proj_left"], tn(attended, rankp_ref[...]))
    packing.put_columns(pack_ref, PROJ_UNITS["proj_right"], SCALING * tn(low, g_ref[...]))
    projected = nn(attended, wp_ref[...]) + SCALING * nn(low, rp_ref[...])
    out_ref[...] = (x_ref[...].astype(F32) + projected + shrunk_ref[...]).astype(BF)


def finish_proj(attended, x, g, shrunk, proj_weight, proj_left, proj_right, rank_proj, packing):
    tokens = x.shape[0]
    return pl.pallas_call(
        partial(finish_proj_kernel, packing),
        out_shape=[jax.ShapeDtypeStruct((tokens, D), BF), jax.ShapeDtypeStruct((PROJ_ROWS, RANK), BF)],
        compiler_params=pltpu.CompilerParams(vmem_limit_bytes=WIDE),
        cost_estimate=MUCH,
        name="finish_proj",
    )(attended, x, g, shrunk, proj_weight, proj_left, proj_right, rank_proj)


def gathered(msg_ref):
    pairs, rows, parts, slots, _ = msg_ref.shape
    return jnp.concatenate(
        [msg_ref[pair, :, part].reshape(rows * slots, PAIR) for part in range(parts) for pair in range(pairs)], axis=1
    )


def finish_kernel(
    packing, msg_ref, x_ref, g_ref, gfeed_ref, wj_ref, lj_ref, rj_ref,
    mgain_ref, mshift_ref, fgain_ref, igrad_ref, pack_ref, wj_here, sems,
):
    third = lambda ref, part: ref.at[:, pl.ds(part * D, D)]
    copies = [pltpu.make_async_copy(third(wj_ref, part), third(wj_here, part), sems.at[part]) for part in range(3)]
    for copy in copies:
        copy.start()
    x, g = x_ref[...].astype(F32), g_ref[...]
    hat, scale = normalised(x)
    joined = gathered(msg_ref)
    rank = (SCALING * nt(joined, rj_ref[...])).astype(BF)
    u = (hat * mgain_ref[...] + mshift_ref[...]).astype(BF)
    packing.put_rows(pack_ref, LATE_UNITS["joined_left"], tn(u, rank))
    grad_mixer = nt(rank, lj_ref[...])
    for part in range(3):
        columns = slice(part * D, (part + 1) * D)
        copies[part].wait()
        grad_mixer = grad_mixer + nt(joined[:, columns], wj_here[:, columns])
    grad_feed = gfeed_ref[...]
    mixer_hat, feed_hat = grad_mixer * hat, grad_feed * hat
    sums = [jnp.sum(v, axis=0, keepdims=True) for v in (mixer_hat, grad_mixer, feed_hat, grad_feed)]
    pieces = [v[:, c * RANK : (c + 1) * RANK] for v in sums for c in range(D // RANK)]
    norms = jnp.concatenate(pieces + [jnp.zeros((RANK - len(pieces), RANK), F32)], axis=0)
    packing.put_rows(pack_ref, LATE_UNITS["norms"], norms)
    pulled = grad_mixer * mgain_ref[...] + grad_feed * fgain_ref[...]
    along = jnp.mean(pulled * hat, axis=-1, keepdims=True)
    level = jnp.mean(pulled, axis=-1, keepdims=True)
    igrad_ref[...] = (g.astype(F32) + scale * (pulled - level - hat * along)).astype(BF)


def finish(message, x, g, grad_feed, joined_weight, joined_left, joined_right,
           mixer_gain, mixer_shift, feed_gain, packing):
    tokens = x.shape[0]
    held = pl.BlockSpec(memory_space=pltpu.VMEM)
    return pl.pallas_call(
        partial(finish_kernel, packing),
        in_specs=[held] * 4 + [pl.BlockSpec(memory_space=pl.ANY)] + [held] * 5,
        out_shape=[jax.ShapeDtypeStruct((tokens, D), BF), jax.ShapeDtypeStruct((LATE_ROWS, RANK), BF)],
        scratch_shapes=[pltpu.VMEM((D, 3 * D), BF), pltpu.SemaphoreType.DMA((3,))],
        compiler_params=pltpu.CompilerParams(vmem_limit_bytes=WIDE),
        cost_estimate=MUCH,
        name="finish",
    )(message, x, g, grad_feed, joined_weight, joined_left, joined_right,
      mixer_gain, mixer_shift, feed_gain)


def right_kernel(packing, head_parts, rest_ref, low_ref, pack_ref):
    count, rows, _, slots, _ = rest_ref.shape
    low = low_ref[...].reshape(count * rows * slots, RANK)
    if packing.rows > 3 * RANK:
        pack_ref[...] = jnp.zeros_like(pack_ref)
    for part in range(3):
        value = SCALING * tn(low, rest_ref[:, :, part].reshape(count * rows * slots, PAIR))
        if head_parts > 1:
            moved = pltpu.roll(value, HEAD_DIM, 1)
            value = jnp.where(lax.axis_index("seq") % head_parts == 0, value, moved)
        packing.put_own(pack_ref, part, value.astype(BF))


def right(rest, low, packing, head_parts):
    return pl.pallas_call(
        partial(right_kernel, packing, head_parts),
        out_shape=jax.ShapeDtypeStruct((packing.rows, RANK), BF),
        compiler_params=pltpu.CompilerParams(vmem_limit_bytes=WIDE),
        cost_estimate=MUCH,
        name="right",
    )(rest, low)


def swap(part, bit, size):
    return lax.ppermute(part, ("batch", "seq"), [(i, i ^ bit) for i in range(size)])


def unpack_kernel(units, count, *refs):
    part_refs, out_refs, (pack_ref, sems) = refs[:count], refs[count:-2], refs[-2:]
    copies, row = [], 0
    for place, part_ref in enumerate(part_refs):
        rows = part_ref.shape[0]
        copies.append(pltpu.make_async_copy(part_ref, pack_ref.at[pl.ds(row, rows)], sems.at[place]))
        row += rows
    for copy in copies:
        copy.start()
    for copy in copies:
        copy.wait()
    for (packing, unit, shape, kind), out_ref in zip(units, out_refs):
        if kind == "columns":
            for step in range(shape[1] // RANK):
                out_ref[:, step * RANK : (step + 1) * RANK] = packing.get(pack_ref, unit + step).astype(F32)
        elif kind == "rows":
            for step in range(shape[0] // RANK):
                out_ref[step * RANK : (step + 1) * RANK] = packing.get(pack_ref, unit + step).astype(F32)
        else:
            out_ref[...] = packing.get(pack_ref, unit)[kind * 8 : (kind + 1) * 8].astype(F32)


def unpack(parts, units):
    rows = sum(part.shape[0] for part in parts)
    return pl.pallas_call(
        partial(unpack_kernel, units, len(parts)),
        in_specs=[pl.BlockSpec(memory_space=pl.ANY)] * len(parts),
        out_shape=[jax.ShapeDtypeStruct(shape, F32) for _, _, shape, _ in units],
        scratch_shapes=[pltpu.VMEM((rows, RANK), BF), pltpu.SemaphoreType.DMA((len(parts),))],
        compiler_params=pltpu.CompilerParams(vmem_limit_bytes=WIDE),
        cost_estimate=LITTLE,
        name="unpack",
    )(*parts)


def per_device(
    block_input, doc_lengths, out_grad, joined_weight, proj_weight, expand_weight, shrink_weight,
    joined_left, joined_right, proj_left, proj_right, expand_left, expand_right, shrink_left,
    shrink_right, mixer_gain, mixer_shift, feed_gain, feed_shift,
):
    rows, slots = block_input.shape[:2]
    tokens = rows * slots
    devices, batches = lax.axis_size("seq"), lax.axis_size("batch")
    size = devices * batches
    me = lax.axis_index("seq")
    length = devices * slots
    x = block_input.reshape(tokens, D)
    g = out_grad.reshape(tokens, D)
    mixer_gain, mixer_shift = mixer_gain.reshape(1, D), mixer_shift.reshape(1, D)
    feed_gain, feed_shift = feed_gain.reshape(1, D), feed_shift.reshape(1, D)

    pair_parts = min(devices, PAIRS)
    row_parts = min(devices // pair_parts, rows)
    head_parts = devices // (pair_parts * row_parts)
    my_rows = rows // row_parts
    lanes = PAIR // head_parts

    def bits(first, count):
        return [first + step for step in range(count.bit_length() - 1)]

    seq_bits = bits(0, devices)
    order = bits(len(seq_bits), batches) + seq_bits
    shared = row_parts * head_parts
    own = order[: batches.bit_length() - 1] + bits(0, shared)
    feed_packing = Packing(FEED_ROWS, order)
    right_packing = PairPacking(order, own, seq_bits[shared.bit_length() - 1 :])
    proj_packing, late_packing = Packing(PROJ_ROWS, order[:3]), Packing(LATE_ROWS, order[:3])

    message, low_joined, rank_proj = project(
        x, g, joined_weight, proj_weight, joined_left, joined_right, proj_left, proj_right,
        mixer_gain, mixer_shift, doc_lengths, rows,
    )

    def send(units):
        if row_parts * head_parts > 1:
            units = units.reshape(PAIRS, row_parts, my_rows, 4, slots, head_parts, lanes)
            units = jnp.transpose(units, (0, 1, 5, 2, 3, 4, 6))
        units = units.reshape(devices, my_rows, 4, slots, lanes)
        return lax.all_to_all(units, "seq", 0, 0, tiled=True)

    def send_back(units):
        parts = units.shape[2] if units.ndim == 5 else 1
        units = lax.all_to_all(units[..., :lanes], "seq", 0, 0, tiled=True)
        if row_parts * head_parts > 1:
            units = units.reshape(PAIRS, row_parts, head_parts, my_rows, parts, slots, lanes)
            units = jnp.transpose(units, (0, 1, 3, 4, 5, 2, 6))
            units = units.reshape((PAIRS, rows, parts, slots, PAIR))
            units = units if parts > 1 else units[:, :, 0]
        return units

    arrived = send(message)
    if lanes < PAIR:
        arrived = jnp.pad(arrived, ((0, 0),) * 4 + ((0, PAIR - lanes),))

    shrunk, grad_feed, feed_pack = feed(
        after(x, message), g, expand_weight, shrink_weight, expand_left, expand_right, shrink_left, shrink_right,
        feed_gain, feed_shift, feed_packing,
    )

    part, steps = feed_pack, list(order)
    part = halve(part, steps.pop(0), size)
    low_all = after(jnp.broadcast_to(low_joined, (devices, tokens, RANK)), part)
    low_all = lax.all_to_all(after(low_all, arrived), "seq", 0, 0, tiled=True)
    answer = attend(arrived, doc_lengths, 0, (), row_parts, head_parts)
    part = halve(part, steps.pop(0), size, *answer)
    for row in range(1, my_rows):
        answer = attend(arrived, doc_lengths, row, answer, row_parts, head_parts)
    attended, rest = answer
    while len(steps) > 2:
        part = halve(part, steps.pop(0), size, *answer)
    attended = send_back(after(attended, part, low_all))

    low_all = low_all.reshape(devices, rows, slots, RANK)
    first_row = (me // head_parts) % row_parts * my_rows
    if row_parts > 1:
        low_all = lax.dynamic_slice_in_dim(low_all, first_row, my_rows, 1)
    right_part = right(rest, low_all, right_packing, head_parts)
    part = quarter(part, steps, size, right_part)
    for bit in own:
        right_part = halve(right_part, bit, size)
    stride = part.shape[0] + right_part.shape[0]
    early = jnp.concatenate([part, right_part])
    returned = send_back(after(rest, attended, early))

    output, proj_part = finish_proj(
        attended, x, g, shrunk, proj_weight, proj_left, proj_right, rank_proj, proj_packing
    )
    early = join(everyone(early, steps, size, output))
    early = double(early, order[-3], size)
    for bit in order[:2]:
        proj_part = halve(proj_part, bit, size)
    input_grad, late_part = finish(
        returned, after(x, early), g, grad_feed, joined_weight, joined_left, joined_right,
        mixer_gain, mixer_shift, feed_gain, late_packing,
    )
    proj_part = halve(proj_part, order[2], size, late_part)
    for bit in order[-4:0:-1]:
        early = double(early, bit, size, late_part)
    late_part = after(late_part, early)
    early = [early, swap(early, 1 << order[0], size)]
    feed_packing, right_packing = feed_packing.held(stride, 0), right_packing.held(stride, part.shape[0])
    early_grads = unpack(early, (
        (feed_packing, FEED_UNITS["expand_left"], (D, RANK), "rows"),
        (feed_packing, FEED_UNITS["expand_right"], (RANK, FF), "columns"),
        (feed_packing, FEED_UNITS["shrink_left"], (FF, RANK), "rows"),
        (feed_packing, FEED_UNITS["shrink_right"], (RANK, D), "columns"),
        (right_packing, 0, (RANK, 3 * D), "columns"),
    ))

    for bit in order[:3]:
        late_part = halve(late_part, bit, size)
    stride, first = proj_part.shape[0] + late_part.shape[0], late_part.shape[0]
    late = jnp.concatenate([late_part, proj_part])
    for bit in order[3:-2]:
        late = add_low(late, swap(late, 1 << bit, size))
    whole_late = everyone(late, order[-2:], size, *early_grads)
    late = add_all(whole_late[0], whole_late[1:])
    for bit in order[2:0:-1]:
        late = double(late, bit, size)
    late = [late, swap(late, 1 << order[0], size)]
    late_packing, proj_packing = late_packing.held(stride, 0), proj_packing.held(stride, first)
    late_grads = unpack(late, (
        (late_packing, LATE_UNITS["joined_left"], (D, RANK), "rows"),
        (proj_packing, PROJ_UNITS["proj_left"], (D, RANK), "rows"),
        (proj_packing, PROJ_UNITS["proj_right"], (RANK, D), "columns"),
    ) + tuple((late_packing, LATE_UNITS["norms"], (8, RANK), which) for which in range(4)))
    return (
        output.reshape(rows, slots, D), input_grad.reshape(rows, slots, D),
        late_grads[0], early_grads[4], late_grads[1], late_grads[2],
        early_grads[0], early_grads[1], early_grads[2], early_grads[3],
    ) + tuple(norm.reshape(D) for norm in late_grads[3:])


def solution(mesh):
    act = P("batch", "seq", None)
    return jax.shard_map(
        per_device,
        mesh=mesh,
        in_specs=(act, P("batch", None), act) + (P(),) * 16,
        out_specs=(act, act) + (P(),) * 12,
        check_vma=False,
    )
```

```python
from functools import partial

import jax
import jax.numpy as jnp
from jax import lax
from jax.experimental import pallas as pl
from jax.experimental.pallas import tpu as pltpu
from jax.sharding import PartitionSpec as P

D = 1024
FF = 4096
HEADS = 16
HEAD_DIM = 64
ROT_DIM = 16
RANK = 128
PAIR = 128
PAIRS = 8

EPSILON = 1e-05
SCALING = 0.25
NEGATIVE = -1e30
BF = jnp.bfloat16
F32 = jnp.float32
MIB = 1024 * 1024
WIDE = 63 * MIB
LITTLE = pl.CostEstimate(flops=1, bytes_accessed=1, transcendentals=0)
MUCH = pl.CostEstimate(flops=2 * 10**11, bytes_accessed=1, transcendentals=0)

FEED_UNITS = {"expand_left": 0, "expand_right": 8, "shrink_left": 40, "shrink_right": 72}
FEED_ROWS = 80 * RANK
PROJ_UNITS = {"proj_left": 0, "proj_right": 8}
PROJ_ROWS = 16 * RANK
LATE_UNITS = {"joined_left": 0, "norms": 8}
LATE_ROWS = 9 * RANK


def nn(left, right):
    return lax.dot_general(left, right, (((1,), (0,)), ((), ())), preferred_element_type=F32)


def nt(left, right):
    return lax.dot_general(left, right, (((1,), (1,)), ((), ())), preferred_element_type=F32)


def tn(left, right):
    return lax.dot_general(left, right, (((0,), (0,)), ((), ())), preferred_element_type=F32)


def normalised(values):
    average = jnp.mean(values, axis=-1, keepdims=True)
    centred = values - average
    spread = jnp.mean(centred * centred, axis=-1, keepdims=True)
    scale = lax.rsqrt(spread + EPSILON)
    return centred * scale, scale


def turn(values, cosine, sine):
    lane = lax.broadcasted_iota(jnp.int32, values.shape, 1) % HEAD_DIM
    half = ROT_DIM // 2
    partner = jnp.where(lane < half, pltpu.roll(values, PAIR - half, 1), pltpu.roll(values, half, 1))
    return values * cosine + partner * sine


def document_starts(doc_ref, row, places):
    ending, begins = jnp.int32(0), jnp.zeros_like(places)
    for entry in range(doc_ref.shape[1]):
        ending = ending + doc_ref[row, entry]
        begins = begins + jnp.where(places >= ending, doc_ref[row, entry], 0)
    return begins


def turning(offsets):
    half = ROT_DIM // 2
    index = lax.broadcasted_iota(jnp.int32, (half, 1), 0)
    frequency = jnp.zeros((half, 1), F32)
    for j in range(half):
        frequency = jnp.where(index == j, 10000.0 ** (-2.0 * j / ROT_DIM), frequency)
    angles = offsets.astype(F32) * frequency
    lane = lax.broadcasted_iota(jnp.int32, (half, PAIR), 1) % HEAD_DIM
    here = (lane < ROT_DIM) & (lane % half == lax.broadcasted_iota(jnp.int32, (half, PAIR), 0))
    spread = jnp.where(here, 1.0, 0.0)
    signed = jnp.where(lane < half, -spread, spread)
    exact = partial(
        lax.dot_general, dimension_numbers=(((0,), (0,)), ((), ())),
        precision=lax.Precision.HIGHEST, preferred_element_type=F32,
    )
    cosine = exact(jnp.cos(angles), spread)
    still = lax.broadcasted_iota(jnp.int32, (1, PAIR), 1) % HEAD_DIM >= ROT_DIM
    return cosine + jnp.where(still, 1.0, 0.0), exact(jnp.sin(angles), signed)


def add_low(left, right):
    return (left.astype(F32) + right.astype(F32)).astype(BF)


def after(value, *others):
    return lax.optimization_barrier((value,) + others)[0] if others else value


class Packing:
    def __init__(self, rows, order, stride=None, first=0):
        self.rows, self.order, self.first = rows, order, first
        self.block = rows // 2 ** len(order)
        self.stride = stride or self.block
        self.piece = max(size for size in (16, 32, 64, 128) if self.block % size == 0 and first % size == 0 and self.stride % size == 0)

    def held(self, stride, first):
        return Packing(self.rows, self.order, stride, first)

    def bits(self, block):
        count = len(self.order)
        return [(block >> (count - 1 - step)) & 1 for step in range(count)]

    def place(self, bits):
        place = 0
        for bit, value in zip(self.order, bits):
            place = place * 2 + (value ^ (lax.shift_right_logical(device_number(), bit) & 1))
        return place

    def pieces(self, unit):
        per = self.block // self.piece
        for part in range(RANK // self.piece):
            piece = unit * (RANK // self.piece) + part
            row = self.place(self.bits(piece // per)) * self.stride + self.first + piece % per * self.piece
            yield part * self.piece, pl.multiple_of(row, 16)

    def put(self, ref, unit, value):
        for first, row in self.pieces(unit):
            ref[pl.ds(row, self.piece), :] = value[first : first + self.piece]

    def get(self, ref, unit):
        return jnp.concatenate([ref[pl.ds(row, self.piece), :] for _, row in self.pieces(unit)], axis=0)

    def put_rows(self, ref, unit, matrix):
        matrix = matrix.astype(BF)
        for step in range(matrix.shape[0] // RANK):
            self.put(ref, unit + step, matrix[step * RANK : (step + 1) * RANK])

    def put_columns(self, ref, unit, matrix):
        matrix = matrix.astype(BF)
        for step in range(matrix.shape[1] // RANK):
            self.put(ref, unit + step, matrix[:, step * RANK : (step + 1) * RANK])


class PairPacking(Packing):
    def __init__(self, order, own, pair_bits, stride=None, first=0):
        self.order, self.own, self.pair_bits = order, own, pair_bits
        self.block = -(-3 * RANK // (16 * 2 ** len(own))) * 16
        self.stride, self.first, self.piece = stride or self.block, first, 16
        self.rows = self.block * 2 ** len(own)

    def held(self, stride, first):
        return PairPacking(self.order, self.own, self.pair_bits, stride, first)

    def pieces(self, unit):
        part, pair = divmod(unit, PAIRS)
        for step in range(RANK // 16):
            row = part * RANK + step * 16
            block, inside = divmod(row, self.block)
            inner = dict(zip(self.own, [(block >> (len(self.own) - 1 - k)) & 1 for k in range(len(self.own))]))
            outer = {bit: (pair >> k) & 1 for k, bit in enumerate(self.pair_bits)}
            bits = [inner[bit] if bit in inner else outer[bit] for bit in self.order]
            at = self.place(bits) * self.stride + self.first + inside
            yield step * 16, pl.multiple_of(at, 16)

    def put_own(self, ref, part, value):
        for step in range(RANK // 16):
            block, inside = divmod(part * RANK + step * 16, self.block)
            place = 0
            for k, bit in enumerate(self.own):
                value_bit = (block >> (len(self.own) - 1 - k)) & 1
                place = place * 2 + (value_bit ^ (lax.shift_right_logical(device_number(), bit) & 1))
            at = pl.multiple_of(place * self.block + inside, 16)
            ref[pl.ds(at, 16), :] = value[step * 16 : (step + 1) * 16]


def device_number():
    return lax.axis_index("batch") * lax.axis_size("seq") + lax.axis_index("seq")


def halve(packed, bit, size, *hold):
    half = packed.shape[0] // 2
    return add_low(packed[:half], after(swap(packed[half:], 1 << bit, size), *hold))


def double(packed, bit, size, *hold):
    return jnp.concatenate([packed, after(swap(packed, 1 << bit, size), *hold)])


def join_kernel(*refs):
    *part_refs, out_ref = refs
    for place, part_ref in enumerate(part_refs):
        rows = part_ref.shape[0]
        out_ref[place * rows : (place + 1) * rows] = part_ref[...]


def join(parts):
    rows = sum(part.shape[0] for part in parts)
    return pl.pallas_call(
        join_kernel,
        out_shape=jax.ShapeDtypeStruct((rows, RANK), BF),
        compiler_params=pltpu.CompilerParams(vmem_limit_bytes=WIDE),
        cost_estimate=LITTLE,
        name="join",
    )(*parts)


def masks(pair):
    return [1 << pair[1], 1 << pair[0], (1 << pair[0]) | (1 << pair[1])]


def quarter(packed, pair, size, *hold):
    blocks = packed.reshape(4, packed.shape[0] // 4, RANK)
    others = [swap(blocks[k + 1], mask, size) for k, mask in enumerate(masks(pair))]
    return add_all(blocks[0], [after(other, *hold) for other in others])


def everyone(packed, pair, size, *hold):
    return [packed] + [after(swap(packed, mask, size), *hold) for mask in masks(pair)]


def add_all(first, others):
    total = first.astype(F32)
    for other in others:
        total = total + other.astype(F32)
    return total.astype(BF)


def fetch(pairs, sems):
    copies = [pltpu.make_async_copy(away, here, sems.at[k]) for k, (away, here) in enumerate(pairs)]
    for copy in copies:
        copy.start()
    return copies


def third(ref, part):
    return ref.at[:, pl.ds(part * D, D)]


def project_kernel(
    x_ref, g_ref, wj_ref, wp_ref, lj_ref, rj_ref, lp_ref, rp_ref, gain_ref, shift_ref, doc_ref,
    msg_ref, lows_ref, rank_ref, wj_here, wp_here, sems,
):
    rows, slots = msg_ref.shape[1], msg_ref.shape[3]
    copies = [pltpu.make_async_copy(wp_ref, wp_here, sems.at[3])] + [
        pltpu.make_async_copy(third(wj_ref, part), third(wj_here, part), sems.at[part]) for part in range(3)
    ]
    for copy in copies:
        copy.start()

    def put(place, matrix):
        matrix = matrix.astype(BF)
        for pair in range(PAIRS):
            for row in range(rows):
                msg_ref[pair, row, place] = matrix[row * slots : (row + 1) * slots, pair * PAIR : (pair + 1) * PAIR]

    g = g_ref[...]
    rank = (SCALING * nt(g, rp_ref[...])).astype(BF)
    rank_ref[...] = rank
    hat, _ = normalised(x_ref[...].astype(F32))
    u = (hat * gain_ref[...] + shift_ref[...]).astype(BF)
    low = nn(u, lj_ref[...]).astype(BF)
    lows_ref[...] = jnp.broadcast_to(low, lows_ref.shape)
    places = lax.axis_index("seq") * slots + lax.broadcasted_iota(jnp.int32, (1, slots), 1)
    turns = [turning(places - document_starts(doc_ref, row, places)) for row in range(rows)]
    cosine = jnp.concatenate([pair[0] for pair in turns], axis=0)
    sine = jnp.concatenate([pair[1] for pair in turns], axis=0)
    copies[0].wait()
    put(3, nt(g, wp_here[...]) + nt(rank, lp_ref[...]))
    for part in range(3):
        columns = slice(part * D, (part + 1) * D)
        copies[part + 1].wait()
        result = nn(u, wj_here[:, columns]) + SCALING * nn(low, rj_ref[:, columns])
        if part < 2:
            result = jnp.concatenate(
                [turn(result[:, k * PAIR : (k + 1) * PAIR], cosine, sine) for k in range(PAIRS)], axis=1
            )
        put(part, result)


def project(x, g, joined_weight, proj_weight, joined_left, joined_right, proj_left, proj_right,
            gain, shift, doc_lengths, rows, devices):
    tokens = x.shape[0]
    held = pl.BlockSpec(memory_space=pltpu.VMEM)
    away = pl.BlockSpec(memory_space=pl.ANY)
    return pl.pallas_call(
        project_kernel,
        in_specs=[held, held, away, away] + [held] * 6 + [pl.BlockSpec(memory_space=pltpu.SMEM)],
        out_shape=[
            jax.ShapeDtypeStruct((PAIRS, rows, 4, tokens // rows, PAIR), BF),
            jax.ShapeDtypeStruct((devices, tokens, RANK), BF),
            jax.ShapeDtypeStruct((tokens, RANK), BF),
        ],
        scratch_shapes=[
            pltpu.VMEM((D, 3 * D), BF), pltpu.VMEM((D, D), BF), pltpu.SemaphoreType.DMA((4,)),
        ],
        compiler_params=pltpu.CompilerParams(vmem_limit_bytes=WIDE),
        cost_estimate=LITTLE,
        name="project",
    )(x, g, joined_weight, proj_weight, joined_left, joined_right, proj_left, proj_right, gain, shift, doc_lengths)


def feed_kernel(
    packing, x_ref, g_ref, we_ref, ws_ref, le_ref, re_ref, ls_ref, rs_ref, gain_ref, shift_ref,
    shrunk_ref, gfeed_ref, pack_ref, f_ref, lowe_ref, ranks_ref, lows_ref, ranke_ref,
):
    step = pl.program_id(0)
    width = we_ref.shape[1]

    @pl.when(step == 0)
    def _():
        hat, _ = normalised(x_ref[...].astype(F32))
        f_ref[...] = (hat * gain_ref[...] + shift_ref[...]).astype(BF)
        lowe_ref[...] = nn(f_ref[...], le_ref[...]).astype(BF)
        ranks_ref[...] = (SCALING * nt(g_ref[...], rs_ref[...])).astype(BF)
        lows_ref[...] = jnp.zeros_like(lows_ref)
        ranke_ref[...] = jnp.zeros_like(ranke_ref)
        shrunk_ref[...] = jnp.zeros_like(shrunk_ref)
        gfeed_ref[...] = jnp.zeros_like(gfeed_ref)

    g, f, ranks = g_ref[...], f_ref[...], ranks_ref[...]
    expanded = nn(f, we_ref[...]) + SCALING * nn(lowe_ref[...], re_ref[...])
    bell = 0.5 * (1.0 + lax.erf(expanded * 0.7071067811865476))
    act = (expanded * bell).astype(BF)
    slope = bell + expanded * (0.3989422804014327 * jnp.exp(-0.5 * expanded * expanded))
    lows_ref[...] += nn(act, ls_ref[...])
    shrunk_ref[...] += nn(act, ws_ref[...])
    grad_act = nt(g, ws_ref[...]) + nt(ranks, ls_ref[...])
    grad_expanded = (grad_act * slope).astype(BF)
    gfeed_ref[...] += nt(grad_expanded, we_ref[...])
    ranke_ref[...] += nt(grad_expanded, re_ref[...])
    units = step * (width // RANK)
    packing.put_columns(pack_ref, FEED_UNITS["expand_right"] + units, SCALING * tn(lowe_ref[...], grad_expanded))
    packing.put_rows(pack_ref, FEED_UNITS["shrink_left"] + units, tn(act, ranks))

    @pl.when(step == pl.num_programs(0) - 1)
    def _():
        low = lows_ref[...].astype(BF)
        shrunk_ref[...] += SCALING * nn(low, rs_ref[...])
        packing.put_columns(pack_ref, FEED_UNITS["shrink_right"], SCALING * tn(low, g))
        ranke = (SCALING * ranke_ref[...]).astype(BF)
        gfeed_ref[...] += nt(ranke, le_ref[...])
        packing.put_rows(pack_ref, FEED_UNITS["expand_left"], tn(f, ranke))


def feed(x, g, expand_weight, shrink_weight, expand_left, expand_right, shrink_left, shrink_right, gain, shift, packing):
    tokens = x.shape[0]
    width = 512
    whole = lambda shape: pl.BlockSpec(shape, lambda j: (0,) * len(shape))
    return pl.pallas_call(
        partial(feed_kernel, packing),
        grid=(FF // width,),
        in_specs=[
            whole((tokens, D)), whole((tokens, D)),
            pl.BlockSpec((D, width), lambda j: (0, j)),
            pl.BlockSpec((width, D), lambda j: (j, 0)),
            whole((D, RANK)),
            pl.BlockSpec((RANK, width), lambda j: (0, j)),
            pl.BlockSpec((width, RANK), lambda j: (j, 0)),
            whole((RANK, D)), whole((1, D)), whole((1, D)),
        ],
        out_specs=[whole((tokens, D)), whole((tokens, D)), whole((FEED_ROWS, RANK))],
        out_shape=[
            jax.ShapeDtypeStruct((tokens, D), F32),
            jax.ShapeDtypeStruct((tokens, D), F32),
            jax.ShapeDtypeStruct((FEED_ROWS, RANK), BF),
        ],
        scratch_shapes=[
            pltpu.VMEM((tokens, D), BF),
            pltpu.VMEM((tokens, RANK), BF), pltpu.VMEM((tokens, RANK), BF),
            pltpu.VMEM((tokens, RANK), F32), pltpu.VMEM((tokens, RANK), F32),
        ],
        compiler_params=pltpu.CompilerParams(vmem_limit_bytes=WIDE),
        cost_estimate=LITTLE,
        name="feed",
    )(x, g, expand_weight, shrink_weight, expand_left, expand_right, shrink_left, shrink_right, gain, shift)


def attend_kernel(first_row, my_rows, row_parts, head_parts, msg_ref, doc_ref, *refs):
    out_ref, rest_ref, vt_ref, kt_ref, dk_ref, dv_ref, cos_ref, sin_ref = refs[-8:]
    count, _, _, slots, _ = msg_ref.shape
    length = count * slots
    row = first_row
    if row_parts > 1:
        row = row + (lax.axis_index("seq") // head_parts) % row_parts * my_rows
    places = lax.broadcasted_iota(jnp.int32, (1, length), 1)
    starts = document_starts(doc_ref, row, places)
    cos_ref[...], sin_ref[...] = turning(places - starts)
    keys = msg_ref[:, 0, 1].reshape(length, PAIR)
    values = msg_ref[:, 0, 2].reshape(length, PAIR)
    kt_ref[...] = keys.T
    vt_ref[...] = values.T
    dk_ref[...] = jnp.zeros_like(dk_ref)
    dv_ref[...] = jnp.zeros_like(dv_ref)
    first_head = lax.broadcasted_iota(jnp.int32, (slots, PAIR), 1) < HEAD_DIM
    none = jnp.zeros((slots, PAIR), BF)

    def both(part):
        return jnp.concatenate([jnp.where(first_head, part, none), jnp.where(first_head, none, part)], axis=0)

    def merge(both_t):
        return jnp.concatenate([both_t[:HEAD_DIM, :slots], both_t[HEAD_DIM:, slots:]], axis=0).T

    def front(block):
        here = slice(block * slots, (block + 1) * slots)
        seen = (block + 1) * slots
        query = both(msg_ref[block, 0, 0] * BF(0.125))
        grad = both(msg_ref[block, 0, 3])
        query_t, grad_t = query.T, grad.T
        start = jnp.concatenate([starts[:, here]] * 2, axis=1)
        place = jnp.concatenate([places[:, here]] * 2, axis=1)
        scores = nn(keys[:seen], query_t)
        key_place = lax.broadcasted_iota(jnp.int32, scores.shape, 0)
        allowed = key_place >= start
        if block:
            last = (key_place[-slots:] <= place) & allowed[-slots:]
            scores = jnp.concatenate(
                [jnp.where(allowed[:-slots], scores[:-slots], NEGATIVE), jnp.where(last, scores[-slots:], NEGATIVE)], axis=0
            )
        else:
            scores = jnp.where(allowed & (key_place <= place), scores, NEGATIVE)
        return scores, query, grad_t

    def back(block, scores, query, grad_t):
        here = slice(block * slots, (block + 1) * slots)
        seen = (block + 1) * slots
        top = jnp.max(scores, axis=0, keepdims=True)
        weights = jnp.exp(scores - top)
        inverse = 1.0 / jnp.sum(weights, axis=0, keepdims=True)
        low = weights.astype(BF)
        out_t = nn(vt_ref[:, :seen], low) * inverse
        scaled_t = grad_t.astype(F32) * inverse
        delta = jnp.sum(out_t * scaled_t, axis=0, keepdims=True)
        scaled_t = scaled_t.astype(BF)
        grad_probs = nn(values[:seen], scaled_t)
        grad_scores = (weights * (grad_probs - delta)).astype(BF)
        dv_ref[:seen] += nn(low, scaled_t.T)
        dk_ref[:seen] += nn(grad_scores, query)
        query_grad_t = nn(kt_ref[:, :seen], grad_scores)
        out_ref[block, 0] = merge(out_t).astype(BF)
        query_grad = turn(0.125 * merge(query_grad_t), cos_ref[here], -sin_ref[here])
        rest_ref[block, 0, 0] = query_grad.astype(BF)

    ready = front(0)
    for block in range(count):
        later = front(block + 1) if block + 1 < count else None
        back(block, *ready)
        ready = later
    for block in range(count):
        here = slice(block * slots, (block + 1) * slots)
        rest_ref[block, 0, 1] = turn(dk_ref[here], cos_ref[here], -sin_ref[here]).astype(BF)
        rest_ref[block, 0, 2] = dv_ref[here].astype(BF)


def attend(message, doc_lengths, row, earlier, row_parts, head_parts):
    count, rows, _, slots, _ = message.shape
    length = count * slots
    return pl.pallas_call(
        partial(attend_kernel, row, rows, row_parts, head_parts),
        grid=(1,),
        in_specs=[
            pl.BlockSpec((count, 1, 4, slots, PAIR), lambda r: (0, row, 0, 0, 0)),
            pl.BlockSpec(memory_space=pltpu.SMEM),
        ] + [pl.BlockSpec(memory_space=pl.ANY)] * len(earlier),
        out_specs=[
            pl.BlockSpec((count, 1, slots, PAIR), lambda r: (0, row, 0, 0)),
            pl.BlockSpec((count, 1, 3, slots, PAIR), lambda r: (0, row, 0, 0, 0)),
        ],
        out_shape=[
            jax.ShapeDtypeStruct((count, rows, slots, PAIR), BF),
            jax.ShapeDtypeStruct((count, rows, 3, slots, PAIR), BF),
        ],
        input_output_aliases={2 + k: k for k in range(len(earlier))},
        scratch_shapes=[
            pltpu.VMEM((PAIR, length), BF), pltpu.VMEM((PAIR, length), BF),
            pltpu.VMEM((length, PAIR), F32), pltpu.VMEM((length, PAIR), F32),
            pltpu.VMEM((length, PAIR), F32), pltpu.VMEM((length, PAIR), F32),
        ],
        compiler_params=pltpu.CompilerParams(vmem_limit_bytes=WIDE),
        cost_estimate=LITTLE if row else MUCH,
        name="attend",
    )(message, doc_lengths, *earlier)


def finish_proj_kernel(
    packing, att_ref, x_ref, g_ref, shrunk_ref, wp_ref, lp_ref, rp_ref, rankp_ref, out_ref, pack_ref,
):
    pairs, rows, slots, _ = att_ref.shape
    attended = jnp.concatenate([att_ref[pair].reshape(rows * slots, PAIR) for pair in range(pairs)], axis=1)
    low = nn(attended, lp_ref[...]).astype(BF)
    packing.put_rows(pack_ref, PROJ_UNITS["proj_left"], tn(attended, rankp_ref[...]))
    packing.put_columns(pack_ref, PROJ_UNITS["proj_right"], SCALING * tn(low, g_ref[...]))
    projected = nn(attended, wp_ref[...]) + SCALING * nn(low, rp_ref[...])
    out_ref[...] = (x_ref[...].astype(F32) + projected + shrunk_ref[...]).astype(BF)


def finish_proj(attended, x, g, shrunk, proj_weight, proj_left, proj_right, rank_proj, packing):
    tokens = x.shape[0]
    return pl.pallas_call(
        partial(finish_proj_kernel, packing),
        out_shape=[jax.ShapeDtypeStruct((tokens, D), BF), jax.ShapeDtypeStruct((PROJ_ROWS, RANK), BF)],
        compiler_params=pltpu.CompilerParams(vmem_limit_bytes=WIDE),
        cost_estimate=MUCH,
        name="finish_proj",
    )(attended, x, g, shrunk, proj_weight, proj_left, proj_right, rank_proj)


def gathered(msg_ref):
    pairs, rows, parts, slots, _ = msg_ref.shape
    return jnp.concatenate(
        [msg_ref[pair, :, part].reshape(rows * slots, PAIR) for part in range(parts) for pair in range(pairs)], axis=1
    )


def finish_kernel(
    packing, x_away, msg_away, rj_away, wj_away, lj_away, gfeed_away, g_away,
    mgain_ref, mshift_ref, fgain_ref, igrad_ref, pack_ref,
    x_ref, msg_ref, rj_ref, wj_ref, lj_ref, gfeed_ref, g_ref, sems,
):
    x_in, msg_in, rj_in, w0_in, w1_in, w2_in, lj_in, gfeed_in, g_in = fetch([
        (x_away, x_ref), (msg_away, msg_ref), (rj_away, rj_ref),
    ] + [(third(wj_away, part), third(wj_ref, part)) for part in range(3)] + [
        (lj_away, lj_ref), (gfeed_away, gfeed_ref), (g_away, g_ref),
    ], sems)
    x_in.wait()
    hat, scale = normalised(x_ref[...].astype(F32))
    u = (hat * mgain_ref[...] + mshift_ref[...]).astype(BF)
    msg_in.wait()
    rj_in.wait()
    joined = gathered(msg_ref)
    rank = (SCALING * nt(joined, rj_ref[...])).astype(BF)
    packing.put_rows(pack_ref, LATE_UNITS["joined_left"], tn(u, rank))
    grad_mixer = jnp.zeros(hat.shape, F32)
    for part, wait in enumerate((w0_in, w1_in, w2_in)):
        columns = slice(part * D, (part + 1) * D)
        wait.wait()
        grad_mixer = grad_mixer + nt(joined[:, columns], wj_ref[:, columns])
    lj_in.wait()
    grad_mixer = grad_mixer + nt(rank, lj_ref[...])
    gfeed_in.wait()
    g_in.wait()
    g = g_ref[...]
    grad_feed = gfeed_ref[...]
    mixer_hat, feed_hat = grad_mixer * hat, grad_feed * hat
    sums = [jnp.sum(v, axis=0, keepdims=True) for v in (mixer_hat, grad_mixer, feed_hat, grad_feed)]
    pieces = [v[:, c * RANK : (c + 1) * RANK] for v in sums for c in range(D // RANK)]
    norms = jnp.concatenate(pieces + [jnp.zeros((RANK - len(pieces), RANK), F32)], axis=0)
    packing.put_rows(pack_ref, LATE_UNITS["norms"], norms)
    pulled = grad_mixer * mgain_ref[...] + grad_feed * fgain_ref[...]
    along = jnp.mean(pulled * hat, axis=-1, keepdims=True)
    level = jnp.mean(pulled, axis=-1, keepdims=True)
    igrad_ref[...] = (g.astype(F32) + scale * (pulled - level - hat * along)).astype(BF)


def finish(message, x, g, grad_feed, joined_weight, joined_left, joined_right,
           mixer_gain, mixer_shift, feed_gain, packing):
    tokens = x.shape[0]
    held = pl.BlockSpec(memory_space=pltpu.VMEM)
    loads = (x, message, joined_right, joined_weight, joined_left, grad_feed, g)
    return pl.pallas_call(
        partial(finish_kernel, packing),
        in_specs=[pl.BlockSpec(memory_space=pl.ANY)] * len(loads) + [held] * 3,
        out_shape=[jax.ShapeDtypeStruct((tokens, D), BF), jax.ShapeDtypeStruct((LATE_ROWS, RANK), BF)],
        scratch_shapes=[pltpu.VMEM(load.shape, load.dtype) for load in loads] + [pltpu.SemaphoreType.DMA((9,))],
        compiler_params=pltpu.CompilerParams(vmem_limit_bytes=WIDE),
        cost_estimate=MUCH,
        name="finish",
    )(*loads, mixer_gain, mixer_shift, feed_gain)


def right_kernel(packing, head_parts, rest_ref, low_ref, pack_ref):
    count, rows, _, slots, _ = rest_ref.shape
    low = low_ref[...].reshape(count * rows * slots, RANK)
    if packing.rows > 3 * RANK:
        pack_ref[...] = jnp.zeros_like(pack_ref)
    for part in range(3):
        value = SCALING * tn(low, rest_ref[:, :, part].reshape(count * rows * slots, PAIR))
        if head_parts > 1:
            moved = pltpu.roll(value, HEAD_DIM, 1)
            value = jnp.where(lax.axis_index("seq") % head_parts == 0, value, moved)
        packing.put_own(pack_ref, part, value.astype(BF))


def right(rest, low, packing, head_parts):
    return pl.pallas_call(
        partial(right_kernel, packing, head_parts),
        out_shape=jax.ShapeDtypeStruct((packing.rows, RANK), BF),
        compiler_params=pltpu.CompilerParams(vmem_limit_bytes=WIDE),
        cost_estimate=MUCH,
        name="right",
    )(rest, low)


def swap(part, bit, size):
    return lax.ppermute(part, ("batch", "seq"), [(i, i ^ bit) for i in range(size)])


def unpack_kernel(units, count, *refs):
    part_refs, out_refs, refs = refs[:count], refs[count : count + len(units)], refs[count + len(units) :]
    value_refs, (pack_ref, sems, out_sems) = refs[:-3], refs[-3:]
    rows = part_refs[0].shape[0]
    for copy in fetch([(ref, pack_ref.at[pl.ds(k * rows, rows)]) for k, ref in enumerate(part_refs)], sems):
        copy.wait()
    outs = []
    for (packing, unit, shape, kind), out_ref, value_ref in zip(units, out_refs, value_refs):
        if kind == "columns":
            for step in range(shape[1] // RANK):
                value_ref[:, step * RANK : (step + 1) * RANK] = packing.get(pack_ref, unit + step).astype(F32)
        elif kind == "rows":
            for step in range(shape[0] // RANK):
                value_ref[step * RANK : (step + 1) * RANK] = packing.get(pack_ref, unit + step).astype(F32)
        else:
            value_ref[...] = packing.get(pack_ref, unit)[kind * 8 : (kind + 1) * 8].astype(F32)
        outs.append(pltpu.make_async_copy(value_ref, out_ref, out_sems.at[len(outs)]))
        outs[-1].start()
    for out in outs:
        out.wait()


def unpack(parts, units):
    rows = sum(part.shape[0] for part in parts)
    away = pl.BlockSpec(memory_space=pl.ANY)
    return pl.pallas_call(
        partial(unpack_kernel, units, len(parts)),
        in_specs=[away] * len(parts),
        out_specs=[away] * len(units),
        out_shape=[jax.ShapeDtypeStruct(shape, F32) for _, _, shape, _ in units],
        scratch_shapes=[pltpu.VMEM(shape, F32) for _, _, shape, _ in units] + [
            pltpu.VMEM((rows, RANK), BF),
            pltpu.SemaphoreType.DMA((len(parts),)), pltpu.SemaphoreType.DMA((len(units),)),
        ],
        compiler_params=pltpu.CompilerParams(vmem_limit_bytes=WIDE),
        cost_estimate=LITTLE,
        name="unpack",
    )(*parts)


def per_device(
    block_input, doc_lengths, out_grad, joined_weight, proj_weight, expand_weight, shrink_weight,
    joined_left, joined_right, proj_left, proj_right, expand_left, expand_right, shrink_left,
    shrink_right, mixer_gain, mixer_shift, feed_gain, feed_shift,
):
    rows, slots = block_input.shape[:2]
    tokens = rows * slots
    devices, batches = lax.axis_size("seq"), lax.axis_size("batch")
    size = devices * batches
    me = lax.axis_index("seq")
    length = devices * slots
    x = block_input.reshape(tokens, D)
    g = out_grad.reshape(tokens, D)
    mixer_gain, mixer_shift = mixer_gain.reshape(1, D), mixer_shift.reshape(1, D)
    feed_gain, feed_shift = feed_gain.reshape(1, D), feed_shift.reshape(1, D)

    pair_parts = min(devices, PAIRS)
    row_parts = min(devices // pair_parts, rows)
    head_parts = devices // (pair_parts * row_parts)
    my_rows = rows // row_parts
    lanes = PAIR // head_parts

    def bits(first, count):
        return [first + step for step in range(count.bit_length() - 1)]

    seq_bits = bits(0, devices)
    batch_bits = bits(len(seq_bits), batches)
    order = batch_bits[:1] + seq_bits[:1] + batch_bits[1:] + seq_bits[1:]
    late_order = [order[0], order[2], order[1]]
    shared = row_parts * head_parts
    own = batch_bits + bits(0, shared)
    feed_packing = Packing(FEED_ROWS, order)
    right_packing = PairPacking(order, own, seq_bits[shared.bit_length() - 1 :])
    proj_packing, late_packing = Packing(PROJ_ROWS, late_order), Packing(LATE_ROWS, late_order)

    message, lows, rank_proj = project(
        x, g, joined_weight, proj_weight, joined_left, joined_right, proj_left, proj_right,
        mixer_gain, mixer_shift, doc_lengths, rows, devices,
    )

    def send(units):
        if row_parts * head_parts > 1:
            units = units.reshape(PAIRS, row_parts, my_rows, 4, slots, head_parts, lanes)
            units = jnp.transpose(units, (0, 1, 5, 2, 3, 4, 6))
        units = units.reshape(devices, my_rows, 4, slots, lanes)
        return lax.all_to_all(units, "seq", 0, 0, tiled=True)

    def send_back(units):
        parts = units.shape[2] if units.ndim == 5 else 1
        units = lax.all_to_all(units[..., :lanes], "seq", 0, 0, tiled=True)
        if row_parts * head_parts > 1:
            units = units.reshape(PAIRS, row_parts, head_parts, my_rows, parts, slots, lanes)
            units = jnp.transpose(units, (0, 1, 3, 4, 5, 2, 6))
            units = units.reshape((PAIRS, rows, parts, slots, PAIR))
            units = units if parts > 1 else units[:, :, 0]
        return units

    arrived = send(message)
    if lanes < PAIR:
        arrived = jnp.pad(arrived, ((0, 0),) * 4 + ((0, PAIR - lanes),))

    shrunk, grad_feed, feed_pack = feed(
        after(x, message), g, expand_weight, shrink_weight, expand_left, expand_right, shrink_left, shrink_right,
        feed_gain, feed_shift, feed_packing,
    )

    part, steps = feed_pack, list(order)
    part = halve(part, steps.pop(0), size)
    low_all = lax.all_to_all(after(lows, arrived), "seq", 0, 0, tiled=True)
    answer = attend(arrived, doc_lengths, 0, (), row_parts, head_parts)
    part = halve(part, steps.pop(0), size, *answer)
    for row in range(1, my_rows):
        answer = attend(arrived, doc_lengths, row, answer, row_parts, head_parts)
    attended, rest = answer
    while len(steps) > 2:
        part = halve(part, steps.pop(0), size, *answer)
    attended = send_back(after(attended, part, low_all))

    low_all = low_all.reshape(devices, rows, slots, RANK)
    first_row = (me // head_parts) % row_parts * my_rows
    if row_parts > 1:
        low_all = lax.dynamic_slice_in_dim(low_all, first_row, my_rows, 1)
    right_part = right(rest, low_all, right_packing, head_parts)
    part = quarter(part, steps, size, right_part)
    for bit in own:
        right_part = halve(right_part, bit, size)
    stride = part.shape[0] + right_part.shape[0]
    early = jnp.concatenate([part, right_part])
    returned = send_back(after(rest, attended, early))

    output, proj_part = finish_proj(
        attended, x, g, shrunk, proj_weight, proj_left, proj_right, rank_proj, proj_packing
    )
    early = join(everyone(early, steps, size, output))
    early = double(early, order[-3], size)
    for bit in late_order[:2]:
        proj_part = halve(proj_part, bit, size)
    input_grad, late_part = finish(
        returned, after(x, early), g, grad_feed, joined_weight, joined_left, joined_right,
        mixer_gain, mixer_shift, feed_gain, late_packing,
    )
    proj_part = halve(proj_part, late_order[2], size, late_part)
    for bit in order[-4:0:-1]:
        early = double(early, bit, size, late_part)
    late_part = after(late_part, early)
    early = [early, swap(early, 1 << order[0], size)]
    feed_packing, right_packing = feed_packing.held(stride, 0), right_packing.held(stride, part.shape[0])
    early_grads = unpack(early, (
        (feed_packing, FEED_UNITS["expand_left"], (D, RANK), "rows"),
        (feed_packing, FEED_UNITS["expand_right"], (RANK, FF), "columns"),
        (feed_packing, FEED_UNITS["shrink_left"], (FF, RANK), "rows"),
        (feed_packing, FEED_UNITS["shrink_right"], (RANK, D), "columns"),
        (right_packing, 0, (RANK, 3 * D), "columns"),
    ))

    for bit in late_order:
        late_part = halve(late_part, bit, size)
    stride, first = proj_part.shape[0] + late_part.shape[0], late_part.shape[0]
    late = jnp.concatenate([late_part, proj_part])
    for bit in order[3:-2]:
        late = add_low(late, swap(late, 1 << bit, size))
    whole_late = everyone(late, order[-2:], size, *early_grads)
    late = add_all(whole_late[0], whole_late[1:])
    for bit in late_order[:0:-1]:
        late = double(late, bit, size)
    late = [late, swap(late, 1 << order[0], size)]
    late_packing, proj_packing = late_packing.held(stride, 0), proj_packing.held(stride, first)
    late_grads = unpack(late, (
        (late_packing, LATE_UNITS["joined_left"], (D, RANK), "rows"),
        (proj_packing, PROJ_UNITS["proj_left"], (D, RANK), "rows"),
        (proj_packing, PROJ_UNITS["proj_right"], (RANK, D), "columns"),
    ) + tuple((late_packing, LATE_UNITS["norms"], (8, RANK), which) for which in range(4)))
    return (
        output.reshape(rows, slots, D), input_grad.reshape(rows, slots, D),
        late_grads[0], early_grads[4], late_grads[1], late_grads[2],
        early_grads[0], early_grads[1], early_grads[2], early_grads[3],
    ) + tuple(norm.reshape(D) for norm in late_grads[3:])


def solution(mesh):
    act = P("batch", "seq", None)
    return jax.shard_map(
        per_device,
        mesh=mesh,
        in_specs=(act, P("batch", None), act) + (P(),) * 16,
        out_specs=(act, act) + (P(),) * 12,
        check_vma=False,
    )
```

```python
from functools import partial

import jax
import jax.numpy as jnp
from jax import lax
from jax.experimental import pallas as pl
from jax.experimental.pallas import tpu as pltpu
from jax.sharding import PartitionSpec as P

D = 1024
FF = 4096
HEADS = 16
HEAD_DIM = 64
ROT_DIM = 16
RANK = 128
PAIR = 128
PAIRS = 8

EPSILON = 1e-05
SCALING = 0.25
NEGATIVE = -1e30
BF = jnp.bfloat16
F32 = jnp.float32
MIB = 1024 * 1024
WIDE = 63 * MIB
LITTLE = pl.CostEstimate(flops=1, bytes_accessed=1, transcendentals=0)
MUCH = pl.CostEstimate(flops=2 * 10**11, bytes_accessed=1, transcendentals=0)

FEED_UNITS = {"expand_left": 0, "expand_right": 8, "shrink_left": 40, "shrink_right": 72}
FEED_ROWS = 80 * RANK
PROJ_UNITS = {"proj_left": 0, "proj_right": 8}
PROJ_ROWS = 16 * RANK
LATE_UNITS = {"joined_left": 0, "norms": 8}
LATE_ROWS = 9 * RANK


def nn(left, right):
    return lax.dot_general(left, right, (((1,), (0,)), ((), ())), preferred_element_type=F32)


def nt(left, right):
    return lax.dot_general(left, right, (((1,), (1,)), ((), ())), preferred_element_type=F32)


def tn(left, right):
    return lax.dot_general(left, right, (((0,), (0,)), ((), ())), preferred_element_type=F32)


def normalised(values):
    average = jnp.mean(values, axis=-1, keepdims=True)
    centred = values - average
    spread = jnp.mean(centred * centred, axis=-1, keepdims=True)
    scale = lax.rsqrt(spread + EPSILON)
    return centred * scale, scale


def turn(values, cosine, sine):
    lane = lax.broadcasted_iota(jnp.int32, values.shape, 1) % HEAD_DIM
    half = ROT_DIM // 2
    partner = jnp.where(lane < half, pltpu.roll(values, PAIR - half, 1), pltpu.roll(values, half, 1))
    return values * cosine + partner * sine


def document_starts(doc_ref, row, places):
    ending, begins = jnp.int32(0), jnp.zeros_like(places)
    for entry in range(doc_ref.shape[1]):
        ending = ending + doc_ref[row, entry]
        begins = begins + jnp.where(places >= ending, doc_ref[row, entry], 0)
    return begins


def turning(offsets):
    half = ROT_DIM // 2
    index = lax.broadcasted_iota(jnp.int32, (half, 1), 0)
    frequency = jnp.zeros((half, 1), F32)
    for j in range(half):
        frequency = jnp.where(index == j, 10000.0 ** (-2.0 * j / ROT_DIM), frequency)
    angles = offsets.astype(F32) * frequency
    lane = lax.broadcasted_iota(jnp.int32, (half, PAIR), 1) % HEAD_DIM
    here = (lane < ROT_DIM) & (lane % half == lax.broadcasted_iota(jnp.int32, (half, PAIR), 0))
    spread = jnp.where(here, 1.0, 0.0)
    signed = jnp.where(lane < half, -spread, spread)
    exact = partial(
        lax.dot_general, dimension_numbers=(((0,), (0,)), ((), ())),
        precision=lax.Precision.HIGHEST, preferred_element_type=F32,
    )
    cosine = exact(jnp.cos(angles), spread)
    still = lax.broadcasted_iota(jnp.int32, (1, PAIR), 1) % HEAD_DIM >= ROT_DIM
    return cosine + jnp.where(still, 1.0, 0.0), exact(jnp.sin(angles), signed)


def add_low(left, right):
    return (left.astype(F32) + right.astype(F32)).astype(BF)


def after(value, *others):
    return lax.optimization_barrier((value,) + others)[0] if others else value


class Packing:
    def __init__(self, rows, order, stride=None, first=0):
        self.rows, self.order, self.first = rows, order, first
        self.block = rows // 2 ** len(order)
        self.stride = stride or self.block
        self.piece = max(size for size in (16, 32, 64, 128) if self.block % size == 0 and first % size == 0 and self.stride % size == 0)

    def held(self, stride, first):
        return Packing(self.rows, self.order, stride, first)

    def bits(self, block):
        count = len(self.order)
        return [(block >> (count - 1 - step)) & 1 for step in range(count)]

    def place(self, bits):
        place = 0
        for bit, value in zip(self.order, bits):
            place = place * 2 + (value ^ (lax.shift_right_logical(device_number(), bit) & 1))
        return place

    def pieces(self, unit):
        per = self.block // self.piece
        for part in range(RANK // self.piece):
            piece = unit * (RANK // self.piece) + part
            row = self.place(self.bits(piece // per)) * self.stride + self.first + piece % per * self.piece
            yield part * self.piece, pl.multiple_of(row, 16)

    def put(self, ref, unit, value):
        for first, row in self.pieces(unit):
            ref[pl.ds(row, self.piece), :] = value[first : first + self.piece]

    def get(self, ref, unit):
        return jnp.concatenate([ref[pl.ds(row, self.piece), :] for _, row in self.pieces(unit)], axis=0)

    def put_rows(self, ref, unit, matrix):
        matrix = matrix.astype(BF)
        for step in range(matrix.shape[0] // RANK):
            self.put(ref, unit + step, matrix[step * RANK : (step + 1) * RANK])

    def put_columns(self, ref, unit, matrix):
        matrix = matrix.astype(BF)
        for step in range(matrix.shape[1] // RANK):
            self.put(ref, unit + step, matrix[:, step * RANK : (step + 1) * RANK])


class PairPacking(Packing):
    def __init__(self, order, own, pair_bits, stride=None, first=0):
        self.order, self.own, self.pair_bits = order, own, pair_bits
        self.block = -(-3 * RANK // (16 * 2 ** len(own))) * 16
        self.stride, self.first, self.piece = stride or self.block, first, 16
        self.rows = self.block * 2 ** len(own)

    def held(self, stride, first):
        return PairPacking(self.order, self.own, self.pair_bits, stride, first)

    def pieces(self, unit):
        part, pair = divmod(unit, PAIRS)
        for step in range(RANK // 16):
            row = part * RANK + step * 16
            block, inside = divmod(row, self.block)
            inner = dict(zip(self.own, [(block >> (len(self.own) - 1 - k)) & 1 for k in range(len(self.own))]))
            outer = {bit: (pair >> k) & 1 for k, bit in enumerate(self.pair_bits)}
            bits = [inner[bit] if bit in inner else outer[bit] for bit in self.order]
            at = self.place(bits) * self.stride + self.first + inside
            yield step * 16, pl.multiple_of(at, 16)

    def put_own(self, ref, part, value):
        for step in range(RANK // 16):
            block, inside = divmod(part * RANK + step * 16, self.block)
            place = 0
            for k, bit in enumerate(self.own):
                value_bit = (block >> (len(self.own) - 1 - k)) & 1
                place = place * 2 + (value_bit ^ (lax.shift_right_logical(device_number(), bit) & 1))
            at = pl.multiple_of(place * self.block + inside, 16)
            ref[pl.ds(at, 16), :] = value[step * 16 : (step + 1) * 16]


def device_number():
    return lax.axis_index("batch") * lax.axis_size("seq") + lax.axis_index("seq")


def halve(packed, bit, size, *hold):
    half = packed.shape[0] // 2
    return add_low(packed[:half], after(swap(packed[half:], 1 << bit, size), *hold))


def double(packed, bit, size, *hold):
    return jnp.concatenate([packed, after(swap(packed, 1 << bit, size), *hold)])


def last_two(packed, bit, last_bit, size):
    parts = [packed, swap(packed, 1 << bit, size)]
    return parts + [swap(part, 1 << last_bit, size) for part in parts]


def join_kernel(*refs):
    *part_refs, out_ref = refs
    for place, part_ref in enumerate(part_refs):
        rows = part_ref.shape[0]
        out_ref[place * rows : (place + 1) * rows] = part_ref[...]


def join(parts):
    rows = sum(part.shape[0] for part in parts)
    return pl.pallas_call(
        join_kernel,
        out_shape=jax.ShapeDtypeStruct((rows, RANK), BF),
        compiler_params=pltpu.CompilerParams(vmem_limit_bytes=WIDE),
        cost_estimate=LITTLE,
        name="join",
    )(*parts)


def masks(pair):
    return [1 << pair[1], 1 << pair[0], (1 << pair[0]) | (1 << pair[1])]


def fold_kernel(keep_ref, other_ref, *block_refs):
    rows = block_refs[0].shape[0]
    for place, block_ref in enumerate(block_refs):
        here = slice(place * rows, (place + 1) * rows)
        block_ref[...] = (keep_ref[here].astype(F32) + other_ref[here].astype(F32)).astype(BF)


def fold(packed, bit, size, *hold):
    half = packed.shape[0] // 2
    other = after(swap(packed[half:], 1 << bit, size), *hold)
    return pl.pallas_call(
        fold_kernel,
        grid=(1,),
        in_specs=[pl.BlockSpec((half, RANK), lambda j: (0, 0))] * 2,
        out_specs=[pl.BlockSpec((half // 4, RANK), lambda j: (0, 0))] * 4,
        out_shape=[jax.ShapeDtypeStruct((half // 4, RANK), BF)] * 4,
        compiler_params=pltpu.CompilerParams(vmem_limit_bytes=WIDE),
        cost_estimate=LITTLE,
        name="fold",
    )(packed, other)


def quarter(blocks, pair, size, *hold):
    others = [swap(blocks[k + 1], mask, size) for k, mask in enumerate(masks(pair))]
    return add_all(blocks[0], [after(other, *hold) for other in others])


def everyone(packed, pair, size, *hold):
    return [packed] + [after(swap(packed, mask, size), *hold) for mask in masks(pair)]


def add_all(first, others):
    total = first.astype(F32)
    for other in others:
        total = total + other.astype(F32)
    return total.astype(BF)


def fetch(pairs, sems):
    copies = [pltpu.make_async_copy(away, here, sems.at[k]) for k, (away, here) in enumerate(pairs)]
    for copy in copies:
        copy.start()
    return copies


def third(ref, part):
    return ref.at[:, pl.ds(part * D, D)]


def project_kernel(
    x_ref, g_ref, wj_ref, wp_ref, lj_ref, rj_ref, lp_ref, rp_ref, gain_ref, shift_ref, doc_ref,
    msg_ref, lows_ref, rank_ref, wj_here, wp_here, sems,
):
    rows, slots = msg_ref.shape[1], msg_ref.shape[3]
    copies = [pltpu.make_async_copy(wp_ref, wp_here, sems.at[3])] + [
        pltpu.make_async_copy(third(wj_ref, part), third(wj_here, part), sems.at[part]) for part in range(3)
    ]
    for copy in copies:
        copy.start()

    def put(place, matrix):
        matrix = matrix.astype(BF)
        for pair in range(PAIRS):
            for row in range(rows):
                msg_ref[pair, row, place] = matrix[row * slots : (row + 1) * slots, pair * PAIR : (pair + 1) * PAIR]

    g = g_ref[...]
    rank = (SCALING * nt(g, rp_ref[...])).astype(BF)
    rank_ref[...] = rank
    hat, _ = normalised(x_ref[...].astype(F32))
    u = (hat * gain_ref[...] + shift_ref[...]).astype(BF)
    low = nn(u, lj_ref[...]).astype(BF)
    lows_ref[...] = jnp.broadcast_to(low, lows_ref.shape)
    places = lax.axis_index("seq") * slots + lax.broadcasted_iota(jnp.int32, (1, slots), 1)
    turns = [turning(places - document_starts(doc_ref, row, places)) for row in range(rows)]
    cosine = jnp.concatenate([pair[0] for pair in turns], axis=0)
    sine = jnp.concatenate([pair[1] for pair in turns], axis=0)
    copies[0].wait()
    put(3, nt(g, wp_here[...]) + nt(rank, lp_ref[...]))
    for part in range(3):
        columns = slice(part * D, (part + 1) * D)
        copies[part + 1].wait()
        result = nn(u, wj_here[:, columns]) + SCALING * nn(low, rj_ref[:, columns])
        if part < 2:
            result = jnp.concatenate(
                [turn(result[:, k * PAIR : (k + 1) * PAIR], cosine, sine) for k in range(PAIRS)], axis=1
            )
        put(part, result)


def project(x, g, joined_weight, proj_weight, joined_left, joined_right, proj_left, proj_right,
            gain, shift, doc_lengths, rows, devices):
    tokens = x.shape[0]
    held = pl.BlockSpec(memory_space=pltpu.VMEM)
    away = pl.BlockSpec(memory_space=pl.ANY)
    return pl.pallas_call(
        project_kernel,
        in_specs=[held, held, away, away] + [held] * 6 + [pl.BlockSpec(memory_space=pltpu.SMEM)],
        out_shape=[
            jax.ShapeDtypeStruct((PAIRS, rows, 4, tokens // rows, PAIR), BF),
            jax.ShapeDtypeStruct((devices, tokens, RANK), BF),
            jax.ShapeDtypeStruct((tokens, RANK), BF),
        ],
        scratch_shapes=[
            pltpu.VMEM((D, 3 * D), BF), pltpu.VMEM((D, D), BF), pltpu.SemaphoreType.DMA((4,)),
        ],
        compiler_params=pltpu.CompilerParams(vmem_limit_bytes=WIDE),
        cost_estimate=LITTLE,
        name="project",
    )(x, g, joined_weight, proj_weight, joined_left, joined_right, proj_left, proj_right, gain, shift, doc_lengths)


def feed_kernel(
    packing, x_ref, g_ref, we_ref, ws_ref, le_ref, re_ref, ls_ref, rs_ref, gain_ref, shift_ref,
    shrunk_ref, gfeed_ref, pack_ref, f_ref, lowe_ref, ranks_ref, lows_ref, ranke_ref,
):
    step = pl.program_id(0)
    width = we_ref.shape[1]

    @pl.when(step == 0)
    def _():
        hat, _ = normalised(x_ref[...].astype(F32))
        f_ref[...] = (hat * gain_ref[...] + shift_ref[...]).astype(BF)
        lowe_ref[...] = nn(f_ref[...], le_ref[...]).astype(BF)
        ranks_ref[...] = (SCALING * nt(g_ref[...], rs_ref[...])).astype(BF)
        lows_ref[...] = jnp.zeros_like(lows_ref)
        ranke_ref[...] = jnp.zeros_like(ranke_ref)
        shrunk_ref[...] = jnp.zeros_like(shrunk_ref)
        gfeed_ref[...] = jnp.zeros_like(gfeed_ref)

    g, f, ranks = g_ref[...], f_ref[...], ranks_ref[...]
    expanded = nn(f, we_ref[...]) + SCALING * nn(lowe_ref[...], re_ref[...])
    bell = 0.5 * (1.0 + lax.erf(expanded * 0.7071067811865476))
    act = (expanded * bell).astype(BF)
    slope = bell + expanded * (0.3989422804014327 * jnp.exp(-0.5 * expanded * expanded))
    lows_ref[...] += nn(act, ls_ref[...])
    shrunk_ref[...] += nn(act, ws_ref[...])
    grad_act = nt(g, ws_ref[...]) + nt(ranks, ls_ref[...])
    grad_expanded = (grad_act * slope).astype(BF)
    gfeed_ref[...] += nt(grad_expanded, we_ref[...])
    ranke_ref[...] += nt(grad_expanded, re_ref[...])
    units = step * (width // RANK)
    packing.put_columns(pack_ref, FEED_UNITS["expand_right"] + units, SCALING * tn(lowe_ref[...], grad_expanded))
    packing.put_rows(pack_ref, FEED_UNITS["shrink_left"] + units, tn(act, ranks))

    @pl.when(step == pl.num_programs(0) - 1)
    def _():
        low = lows_ref[...].astype(BF)
        shrunk_ref[...] += SCALING * nn(low, rs_ref[...])
        packing.put_columns(pack_ref, FEED_UNITS["shrink_right"], SCALING * tn(low, g))
        ranke = (SCALING * ranke_ref[...]).astype(BF)
        gfeed_ref[...] += nt(ranke, le_ref[...])
        packing.put_rows(pack_ref, FEED_UNITS["expand_left"], tn(f, ranke))


def feed(x, g, expand_weight, shrink_weight, expand_left, expand_right, shrink_left, shrink_right, gain, shift, packing):
    tokens = x.shape[0]
    width = 512
    whole = lambda shape: pl.BlockSpec(shape, lambda j: (0,) * len(shape))
    return pl.pallas_call(
        partial(feed_kernel, packing),
        grid=(FF // width,),
        in_specs=[
            whole((tokens, D)), whole((tokens, D)),
            pl.BlockSpec((D, width), lambda j: (0, j)),
            pl.BlockSpec((width, D), lambda j: (j, 0)),
            whole((D, RANK)),
            pl.BlockSpec((RANK, width), lambda j: (0, j)),
            pl.BlockSpec((width, RANK), lambda j: (j, 0)),
            whole((RANK, D)), whole((1, D)), whole((1, D)),
        ],
        out_specs=[whole((tokens, D)), whole((tokens, D)), whole((FEED_ROWS, RANK))],
        out_shape=[
            jax.ShapeDtypeStruct((tokens, D), F32),
            jax.ShapeDtypeStruct((tokens, D), F32),
            jax.ShapeDtypeStruct((FEED_ROWS, RANK), BF),
        ],
        scratch_shapes=[
            pltpu.VMEM((tokens, D), BF),
            pltpu.VMEM((tokens, RANK), BF), pltpu.VMEM((tokens, RANK), BF),
            pltpu.VMEM((tokens, RANK), F32), pltpu.VMEM((tokens, RANK), F32),
        ],
        compiler_params=pltpu.CompilerParams(vmem_limit_bytes=WIDE),
        cost_estimate=LITTLE,
        name="feed",
    )(x, g, expand_weight, shrink_weight, expand_left, expand_right, shrink_left, shrink_right, gain, shift)


def attend_kernel(first_row, my_rows, row_parts, head_parts, msg_ref, doc_ref, *refs):
    out_ref, rest_ref, vt_ref, kt_ref, dk_ref, dv_ref, cos_ref, sin_ref = refs[-8:]
    count, _, _, slots, _ = msg_ref.shape
    length = count * slots
    row = first_row
    if row_parts > 1:
        row = row + (lax.axis_index("seq") // head_parts) % row_parts * my_rows
    places = lax.broadcasted_iota(jnp.int32, (1, length), 1)
    starts = document_starts(doc_ref, row, places)
    cos_ref[...], sin_ref[...] = turning(places - starts)
    keys = msg_ref[:, 0, 1].reshape(length, PAIR)
    values = msg_ref[:, 0, 2].reshape(length, PAIR)
    kt_ref[...] = keys.T
    vt_ref[...] = values.T
    dk_ref[...] = jnp.zeros_like(dk_ref)
    dv_ref[...] = jnp.zeros_like(dv_ref)
    first_head = lax.broadcasted_iota(jnp.int32, (slots, PAIR), 1) < HEAD_DIM
    none = jnp.zeros((slots, PAIR), BF)

    def both(part):
        return jnp.concatenate([jnp.where(first_head, part, none), jnp.where(first_head, none, part)], axis=0)

    def merge(both_t):
        return jnp.concatenate([both_t[:HEAD_DIM, :slots], both_t[HEAD_DIM:, slots:]], axis=0).T

    def front(block):
        here = slice(block * slots, (block + 1) * slots)
        seen = (block + 1) * slots
        query = both(msg_ref[block, 0, 0] * BF(0.125))
        grad = both(msg_ref[block, 0, 3])
        query_t, grad_t = query.T, grad.T
        start = jnp.concatenate([starts[:, here]] * 2, axis=1)
        place = jnp.concatenate([places[:, here]] * 2, axis=1)
        scores = nn(keys[:seen], query_t)
        key_place = lax.broadcasted_iota(jnp.int32, scores.shape, 0)
        allowed = key_place >= start
        if block:
            last = (key_place[-slots:] <= place) & allowed[-slots:]
            scores = jnp.concatenate(
                [jnp.where(allowed[:-slots], scores[:-slots], NEGATIVE), jnp.where(last, scores[-slots:], NEGATIVE)], axis=0
            )
        else:
            scores = jnp.where(allowed & (key_place <= place), scores, NEGATIVE)
        return scores, query, grad_t

    def back(block, scores, query, grad_t):
        here = slice(block * slots, (block + 1) * slots)
        seen = (block + 1) * slots
        top = jnp.max(scores, axis=0, keepdims=True)
        weights = jnp.exp(scores - top)
        inverse = 1.0 / jnp.sum(weights, axis=0, keepdims=True)
        low = weights.astype(BF)
        out_t = nn(vt_ref[:, :seen], low) * inverse
        scaled_t = grad_t.astype(F32) * inverse
        delta = jnp.sum(out_t * scaled_t, axis=0, keepdims=True)
        scaled_t = scaled_t.astype(BF)
        grad_probs = nn(values[:seen], scaled_t)
        grad_scores = (weights * (grad_probs - delta)).astype(BF)
        dv_ref[:seen] += nn(low, scaled_t.T)
        dk_ref[:seen] += nn(grad_scores, query)
        query_grad_t = nn(kt_ref[:, :seen], grad_scores)
        out_ref[block, 0] = merge(out_t).astype(BF)
        query_grad = turn(0.125 * merge(query_grad_t), cos_ref[here], -sin_ref[here])
        rest_ref[block, 0, 0] = query_grad.astype(BF)

    ready = front(0)
    for block in range(count):
        later = front(block + 1) if block + 1 < count else None
        back(block, *ready)
        ready = later
    for block in range(count):
        here = slice(block * slots, (block + 1) * slots)
        rest_ref[block, 0, 1] = turn(dk_ref[here], cos_ref[here], -sin_ref[here]).astype(BF)
        rest_ref[block, 0, 2] = dv_ref[here].astype(BF)


def attend(message, doc_lengths, row, earlier, row_parts, head_parts):
    count, rows, _, slots, _ = message.shape
    length = count * slots
    return pl.pallas_call(
        partial(attend_kernel, row, rows, row_parts, head_parts),
        grid=(1,),
        in_specs=[
            pl.BlockSpec((count, 1, 4, slots, PAIR), lambda r: (0, row, 0, 0, 0)),
            pl.BlockSpec(memory_space=pltpu.SMEM),
        ] + [pl.BlockSpec(memory_space=pl.ANY)] * len(earlier),
        out_specs=[
            pl.BlockSpec((count, 1, slots, PAIR), lambda r: (0, row, 0, 0)),
            pl.BlockSpec((count, 1, 3, slots, PAIR), lambda r: (0, row, 0, 0, 0)),
        ],
        out_shape=[
            jax.ShapeDtypeStruct((count, rows, slots, PAIR), BF),
            jax.ShapeDtypeStruct((count, rows, 3, slots, PAIR), BF),
        ],
        input_output_aliases={2 + k: k for k in range(len(earlier))},
        scratch_shapes=[
            pltpu.VMEM((PAIR, length), BF), pltpu.VMEM((PAIR, length), BF),
            pltpu.VMEM((length, PAIR), F32), pltpu.VMEM((length, PAIR), F32),
            pltpu.VMEM((length, PAIR), F32), pltpu.VMEM((length, PAIR), F32),
        ],
        compiler_params=pltpu.CompilerParams(vmem_limit_bytes=WIDE),
        cost_estimate=LITTLE if row else MUCH,
        name="attend",
    )(message, doc_lengths, *earlier)


def finish_proj_kernel(
    packing, att_ref, x_ref, g_ref, shrunk_ref, wp_ref, lp_ref, rp_ref, rankp_ref, out_ref, pack_ref,
):
    pairs, rows, slots, _ = att_ref.shape
    attended = jnp.concatenate([att_ref[pair].reshape(rows * slots, PAIR) for pair in range(pairs)], axis=1)
    low = nn(attended, lp_ref[...]).astype(BF)
    packing.put_rows(pack_ref, PROJ_UNITS["proj_left"], tn(attended, rankp_ref[...]))
    packing.put_columns(pack_ref, PROJ_UNITS["proj_right"], SCALING * tn(low, g_ref[...]))
    projected = nn(attended, wp_ref[...]) + SCALING * nn(low, rp_ref[...])
    out_ref[...] = (x_ref[...].astype(F32) + projected + shrunk_ref[...]).astype(BF)


def finish_proj(attended, x, g, shrunk, proj_weight, proj_left, proj_right, rank_proj, packing):
    tokens = x.shape[0]
    return pl.pallas_call(
        partial(finish_proj_kernel, packing),
        out_shape=[jax.ShapeDtypeStruct((tokens, D), BF), jax.ShapeDtypeStruct((PROJ_ROWS, RANK), BF)],
        compiler_params=pltpu.CompilerParams(vmem_limit_bytes=WIDE),
        cost_estimate=MUCH,
        name="finish_proj",
    )(attended, x, g, shrunk, proj_weight, proj_left, proj_right, rank_proj)


def gathered(msg_ref):
    pairs, rows, parts, slots, _ = msg_ref.shape
    return jnp.concatenate(
        [msg_ref[pair, :, part].reshape(rows * slots, PAIR) for part in range(parts) for pair in range(pairs)], axis=1
    )


def finish_kernel(
    packing, x_away, msg_away, rj_away, wj_away, lj_away, gfeed_away, g_away,
    mgain_ref, mshift_ref, fgain_ref, igrad_ref, keep_ref, give_ref,
    x_ref, msg_ref, rj_ref, wj_ref, lj_ref, gfeed_ref, g_ref, pack_ref, sems,
):
    x_in, msg_in, rj_in, w0_in, w1_in, w2_in, lj_in, gfeed_in, g_in = fetch([
        (x_away, x_ref), (msg_away, msg_ref), (rj_away, rj_ref),
    ] + [(third(wj_away, part), third(wj_ref, part)) for part in range(3)] + [
        (lj_away, lj_ref), (gfeed_away, gfeed_ref), (g_away, g_ref),
    ], sems)
    x_in.wait()
    hat, scale = normalised(x_ref[...].astype(F32))
    u = (hat * mgain_ref[...] + mshift_ref[...]).astype(BF)
    msg_in.wait()
    rj_in.wait()
    joined = gathered(msg_ref)
    rank = (SCALING * nt(joined, rj_ref[...])).astype(BF)
    packing.put_rows(pack_ref, LATE_UNITS["joined_left"], tn(u, rank))
    grad_mixer = jnp.zeros(hat.shape, F32)
    for part, wait in enumerate((w0_in, w1_in, w2_in)):
        columns = slice(part * D, (part + 1) * D)
        wait.wait()
        grad_mixer = grad_mixer + nt(joined[:, columns], wj_ref[:, columns])
    lj_in.wait()
    grad_mixer = grad_mixer + nt(rank, lj_ref[...])
    gfeed_in.wait()
    g_in.wait()
    g = g_ref[...]
    grad_feed = gfeed_ref[...]
    mixer_hat, feed_hat = grad_mixer * hat, grad_feed * hat
    sums = [jnp.sum(v, axis=0, keepdims=True) for v in (mixer_hat, grad_mixer, feed_hat, grad_feed)]
    pieces = [v[:, c * RANK : (c + 1) * RANK] for v in sums for c in range(D // RANK)]
    norms = jnp.concatenate(pieces + [jnp.zeros((RANK - len(pieces), RANK), F32)], axis=0)
    packing.put_rows(pack_ref, LATE_UNITS["norms"], norms)
    keep_ref[...] = pack_ref[: LATE_ROWS // 2]
    give_ref[...] = pack_ref[LATE_ROWS // 2 :]
    pulled = grad_mixer * mgain_ref[...] + grad_feed * fgain_ref[...]
    along = jnp.mean(pulled * hat, axis=-1, keepdims=True)
    level = jnp.mean(pulled, axis=-1, keepdims=True)
    igrad_ref[...] = (g.astype(F32) + scale * (pulled - level - hat * along)).astype(BF)


def finish(message, x, g, grad_feed, joined_weight, joined_left, joined_right,
           mixer_gain, mixer_shift, feed_gain, packing):
    tokens = x.shape[0]
    held = pl.BlockSpec(memory_space=pltpu.VMEM)
    loads = (x, message, joined_right, joined_weight, joined_left, grad_feed, g)
    return pl.pallas_call(
        partial(finish_kernel, packing),
        in_specs=[pl.BlockSpec(memory_space=pl.ANY)] * len(loads) + [held] * 3,
        out_shape=[jax.ShapeDtypeStruct((tokens, D), BF)] + [jax.ShapeDtypeStruct((LATE_ROWS // 2, RANK), BF)] * 2,
        scratch_shapes=[pltpu.VMEM(load.shape, load.dtype) for load in loads] + [
            pltpu.VMEM((LATE_ROWS, RANK), BF), pltpu.SemaphoreType.DMA((9,)),
        ],
        compiler_params=pltpu.CompilerParams(vmem_limit_bytes=WIDE),
        cost_estimate=MUCH,
        name="finish",
    )(*loads, mixer_gain, mixer_shift, feed_gain)


def right_kernel(packing, head_parts, rest_ref, low_ref, pack_ref):
    count, rows, _, slots, _ = rest_ref.shape
    low = low_ref[...].reshape(count * rows * slots, RANK)
    if packing.rows > 3 * RANK:
        pack_ref[...] = jnp.zeros_like(pack_ref)
    for part in range(3):
        value = SCALING * tn(low, rest_ref[:, :, part].reshape(count * rows * slots, PAIR))
        if head_parts > 1:
            moved = pltpu.roll(value, HEAD_DIM, 1)
            value = jnp.where(lax.axis_index("seq") % head_parts == 0, value, moved)
        packing.put_own(pack_ref, part, value.astype(BF))


def right(rest, low, packing, head_parts):
    return pl.pallas_call(
        partial(right_kernel, packing, head_parts),
        out_shape=jax.ShapeDtypeStruct((packing.rows, RANK), BF),
        compiler_params=pltpu.CompilerParams(vmem_limit_bytes=WIDE),
        cost_estimate=MUCH,
        name="right",
    )(rest, low)


def swap(part, bit, size):
    return lax.ppermute(part, ("batch", "seq"), [(i, i ^ bit) for i in range(size)])


def unpack_kernel(units, count, *refs):
    part_refs, out_refs, refs = refs[:count], refs[count : count + len(units)], refs[count + len(units) :]
    value_refs, (pack_ref, sems, out_sems) = refs[:-3], refs[-3:]
    rows = part_refs[0].shape[0]
    for copy in fetch([(ref, pack_ref.at[pl.ds(k * rows, rows)]) for k, ref in enumerate(part_refs)], sems):
        copy.wait()
    outs = []
    for (packing, unit, shape, kind), out_ref, value_ref in zip(units, out_refs, value_refs):
        if kind == "columns":
            for step in range(shape[1] // RANK):
                value_ref[:, step * RANK : (step + 1) * RANK] = packing.get(pack_ref, unit + step).astype(F32)
        elif kind == "rows":
            for step in range(shape[0] // RANK):
                value_ref[step * RANK : (step + 1) * RANK] = packing.get(pack_ref, unit + step).astype(F32)
        else:
            value_ref[...] = packing.get(pack_ref, unit)[kind * 8 : (kind + 1) * 8].astype(F32)
        outs.append(pltpu.make_async_copy(value_ref, out_ref, out_sems.at[len(outs)]))
        outs[-1].start()
    for out in outs:
        out.wait()


def unpack(parts, units):
    rows = sum(part.shape[0] for part in parts)
    away = pl.BlockSpec(memory_space=pl.ANY)
    return pl.pallas_call(
        partial(unpack_kernel, units, len(parts)),
        in_specs=[away] * len(parts),
        out_specs=[away] * len(units),
        out_shape=[jax.ShapeDtypeStruct(shape, F32) for _, _, shape, _ in units],
        scratch_shapes=[pltpu.VMEM(shape, F32) for _, _, shape, _ in units] + [
            pltpu.VMEM((rows, RANK), BF),
            pltpu.SemaphoreType.DMA((len(parts),)), pltpu.SemaphoreType.DMA((len(units),)),
        ],
        compiler_params=pltpu.CompilerParams(vmem_limit_bytes=WIDE),
        cost_estimate=LITTLE,
        name="unpack",
    )(*parts)


def per_device(
    block_input, doc_lengths, out_grad, joined_weight, proj_weight, expand_weight, shrink_weight,
    joined_left, joined_right, proj_left, proj_right, expand_left, expand_right, shrink_left,
    shrink_right, mixer_gain, mixer_shift, feed_gain, feed_shift,
):
    rows, slots = block_input.shape[:2]
    tokens = rows * slots
    devices, batches = lax.axis_size("seq"), lax.axis_size("batch")
    size = devices * batches
    me = lax.axis_index("seq")
    length = devices * slots
    x = block_input.reshape(tokens, D)
    g = out_grad.reshape(tokens, D)
    mixer_gain, mixer_shift = mixer_gain.reshape(1, D), mixer_shift.reshape(1, D)
    feed_gain, feed_shift = feed_gain.reshape(1, D), feed_shift.reshape(1, D)

    pair_parts = min(devices, PAIRS)
    row_parts = min(devices // pair_parts, rows)
    head_parts = devices // (pair_parts * row_parts)
    my_rows = rows // row_parts
    lanes = PAIR // head_parts

    def bits(first, count):
        return [first + step for step in range(count.bit_length() - 1)]

    seq_bits = bits(0, devices)
    batch_bits = bits(len(seq_bits), batches)
    order = batch_bits[:1] + seq_bits[:1] + batch_bits[1:] + seq_bits[1:]
    late_order = [order[0], order[2], order[1]]
    shared = row_parts * head_parts
    own = batch_bits + bits(0, shared)
    feed_packing = Packing(FEED_ROWS, order)
    right_packing = PairPacking(order, own, seq_bits[shared.bit_length() - 1 :])
    proj_packing, late_packing = Packing(PROJ_ROWS, late_order), Packing(LATE_ROWS, late_order)

    message, lows, rank_proj = project(
        x, g, joined_weight, proj_weight, joined_left, joined_right, proj_left, proj_right,
        mixer_gain, mixer_shift, doc_lengths, rows, devices,
    )

    def send(units):
        if row_parts * head_parts > 1:
            units = units.reshape(PAIRS, row_parts, my_rows, 4, slots, head_parts, lanes)
            units = jnp.transpose(units, (0, 1, 5, 2, 3, 4, 6))
        units = units.reshape(devices, my_rows, 4, slots, lanes)
        return lax.all_to_all(units, "seq", 0, 0, tiled=True)

    def send_back(units):
        parts = units.shape[2] if units.ndim == 5 else 1
        units = lax.all_to_all(units[..., :lanes], "seq", 0, 0, tiled=True)
        if row_parts * head_parts > 1:
            units = units.reshape(PAIRS, row_parts, head_parts, my_rows, parts, slots, lanes)
            units = jnp.transpose(units, (0, 1, 3, 4, 5, 2, 6))
            units = units.reshape((PAIRS, rows, parts, slots, PAIR))
            units = units if parts > 1 else units[:, :, 0]
        return units

    arrived = send(message)
    if lanes < PAIR:
        arrived = jnp.pad(arrived, ((0, 0),) * 4 + ((0, PAIR - lanes),))

    shrunk, grad_feed, feed_pack = feed(
        after(x, message), g, expand_weight, shrink_weight, expand_left, expand_right, shrink_left, shrink_right,
        feed_gain, feed_shift, feed_packing,
    )

    part, steps = feed_pack, list(order)
    part = halve(part, steps.pop(0), size)
    low_all = lax.all_to_all(after(lows, arrived), "seq", 0, 0, tiled=True)
    answer = attend(arrived, doc_lengths, 0, (), row_parts, head_parts)
    part = halve(part, steps.pop(0), size, *answer)
    for row in range(1, my_rows):
        answer = attend(arrived, doc_lengths, row, answer, row_parts, head_parts)
    attended, rest = answer
    while len(steps) > 3:
        part = halve(part, steps.pop(0), size, *answer)
    part = fold(part, steps.pop(0), size, *answer)
    attended = send_back(after(attended, low_all, *part))

    low_all = low_all.reshape(devices, rows, slots, RANK)
    first_row = (me // head_parts) % row_parts * my_rows
    if row_parts > 1:
        low_all = lax.dynamic_slice_in_dim(low_all, first_row, my_rows, 1)
    right_part = right(rest, low_all, right_packing, head_parts)
    part = quarter(part, steps, size, right_part)
    for bit in own:
        right_part = halve(right_part, bit, size)
    stride = part.shape[0] + right_part.shape[0]
    early = jnp.concatenate([part, right_part])
    returned = send_back(after(rest, attended, early))

    output, proj_part = finish_proj(
        attended, x, g, shrunk, proj_weight, proj_left, proj_right, rank_proj, proj_packing
    )
    early = join(everyone(early, steps, size, output))
    early = double(early, order[-3], size)
    proj_part = quarter(jnp.split(proj_part, 4), late_order[:2], size)
    input_grad, late_part, late_give = finish(
        returned, after(x, early, proj_part), g, grad_feed, joined_weight, joined_left, joined_right,
        mixer_gain, mixer_shift, feed_gain, late_packing,
    )
    late_part = add_low(late_part, swap(late_give, 1 << late_order[0], size))
    late_part = halve(late_part, late_order[1], size)
    for bit in order[-4:1:-1]:
        early = double(early, bit, size)
    early = last_two(early, order[1], order[0], size)
    feed_packing, right_packing = feed_packing.held(stride, 0), right_packing.held(stride, part.shape[0])
    early_grads = unpack(early, (
        (feed_packing, FEED_UNITS["expand_left"], (D, RANK), "rows"),
        (feed_packing, FEED_UNITS["expand_right"], (RANK, FF), "columns"),
        (feed_packing, FEED_UNITS["shrink_left"], (FF, RANK), "rows"),
        (feed_packing, FEED_UNITS["shrink_right"], (RANK, D), "columns"),
        (right_packing, 0, (RANK, 3 * D), "columns"),
    ))

    both = [part.reshape(2, part.shape[0] // 2, RANK) for part in (late_part, proj_part)]
    first, stride = both[0].shape[1], both[0].shape[1] + both[1].shape[1]
    given = swap(jnp.concatenate([part[1] for part in both]), 1 << late_order[2], size)
    late = add_low(jnp.concatenate([part[0] for part in both]), given)
    for bit in order[3:-2]:
        late = add_low(late, swap(late, 1 << bit, size))
    whole_late = everyone(late, order[-2:], size, *early_grads)
    late = add_all(whole_late[0], whole_late[1:])
    for bit in late_order[:1:-1]:
        late = double(late, bit, size)
    late = last_two(late, late_order[1], late_order[0], size)
    late_packing, proj_packing = late_packing.held(stride, 0), proj_packing.held(stride, first)
    late_grads = unpack(late, (
        (late_packing, LATE_UNITS["joined_left"], (D, RANK), "rows"),
        (proj_packing, PROJ_UNITS["proj_left"], (D, RANK), "rows"),
        (proj_packing, PROJ_UNITS["proj_right"], (RANK, D), "columns"),
    ) + tuple((late_packing, LATE_UNITS["norms"], (8, RANK), which) for which in range(4)))
    return (
        output.reshape(rows, slots, D), input_grad.reshape(rows, slots, D),
        late_grads[0], early_grads[4], late_grads[1], late_grads[2],
        early_grads[0], early_grads[1], early_grads[2], early_grads[3],
    ) + tuple(norm.reshape(D) for norm in late_grads[3:])


def solution(mesh):
    act = P("batch", "seq", None)
    return jax.shard_map(
        per_device,
        mesh=mesh,
        in_specs=(act, P("batch", None), act) + (P(),) * 16,
        out_specs=(act, act) + (P(),) * 12,
        check_vma=False,
    )
```
